768 devices in a mesh: grp: 16 (over y, core), shard: 48 (over x, z).
Axes of the slice: x: 4, y: 8, z: 12, core: 2. Of those that a mesh axis runs over, the one named last changes fastest.
Arguments:
- events: bfloat16 [98304, 1024], P(('grp', 'shard')), may hold values from -6 to 6
- user_ids: int32 [98304], P(('grp', 'shard')), may hold values from 0 to 191, as said below
- session_break: int32 [98304], P(('grp', 'shard')), may hold values 0 or 1
- in_gain: float32 [1024], replicated, may hold values from 0.1 to 1.9
- in_weight: bfloat16 [1024, 2048], replicated, may hold values from -0.1875 to 0.1875
- decay_rates: float32 [1024], replicated, may hold values from 0.0001 to 0.04
- keep_factor: float32 [1024], replicated, may hold values from 0.4 to 0.8
- out_gain: float32 [1024], replicated, may hold values from 0.1 to 1.9
- out_weight: bfloat16 [1024, 1024], replicated, may hold values from -0.1875 to 0.1875
Outputs:
- mixed: bfloat16 [98304, 1024], P(('grp', 'shard'))
The draws below stay inside these ranges and needn't reach their ends.
Inputs may be any that keep to these rules, and one draw needn't show every extreme that they name: The owner range of an event is user_ids // 4. In every aligned block of 128 rows at most 7 rows share an owner range; in every aligned stretch of 6144 rows one owner range has exactly 7 rows in each of its blocks.
All inputs are finite; a program needn't handle non-finite values. No bound on the sum of `session_break` on one device may be relied on, other than what follows from the above.
Results may differ from the reference program's by a relative error of at most 0.0057.
Values may be sent and summed in bfloat16 or wider, within the bound.
A program may use at most 64 MiB of HBM per device.

```python
import jax
import jax.numpy as jnp
from jax import lax

D = 1024
EV_DEV = 128
U_DEV = 4
WINDOW = 6144
EVENTS = 98304
USERS = 192
CAP = 7


def draw_user_ids(key, part):
    owners = USERS // U_DEV
    groups = EVENTS // WINDOW
    blocks = EVENTS // EV_DEV
    full_owner = jax.random.randint(jax.random.fold_in(key, 1), (groups,), 0, owners)
    full_block = jnp.repeat(full_owner, owners)

    def one_block(block_key, full_dest):
        pool_index = jax.random.permutation(jax.random.fold_in(block_key, 0), (owners - 1) * CAP)[:EV_DEV - CAP]
        other_owner = (full_dest + 1 + pool_index // CAP) % owners
        owner_list = jnp.concatenate([jnp.full((CAP,), full_dest, jnp.int32), other_owner.astype(jnp.int32)])
        shuffle_order = jax.random.permutation(jax.random.fold_in(block_key, 1), EV_DEV)
        owner_list = owner_list[shuffle_order]
        local_user = jax.random.randint(jax.random.fold_in(block_key, 2), (EV_DEV,), 0, U_DEV)
        return (owner_list * U_DEV + local_user).astype(jnp.int32)
    block_keys = jax.random.split(jax.random.fold_in(key, 2), blocks)
    return jax.vmap(one_block)(block_keys, full_block).reshape(EVENTS)


def draw_decay_rates(key, part):
    key_one = jax.random.fold_in(key, 11)
    return jnp.exp(jax.random.uniform(key_one, (D,), jnp.float32, jnp.log(0.001), jnp.log(0.04)))


def place_ends(entries, stream_key, smallest, largest):
    longest = entries.shape.index(max(entries.shape))
    spots = []
    for shift in (0, 1):
        where = [jax.random.randint(jax.random.fold_in(stream_key, axis), (), 0, length) for axis, length in enumerate(entries.shape)]
        where[longest] = (where[longest] + shift) % entries.shape[longest]
        spots.append(tuple(where))
    return entries.at[spots[0]].set(smallest).at[spots[1]].set(largest)


def block_scale(stream_key, shape, shards, smallest, high):
    level = 1.0
    for dim, shards_of in shards:
        heights = jax.random.uniform(jax.random.fold_in(jax.random.fold_in(stream_key, 6), dim), (shards_of,), jnp.float32, smallest / len(shards), high / len(shards))
        level = level * jnp.repeat(jnp.exp(heights), shape[dim] // shards_of).reshape((-1,) + (1,) * (len(shape) - 1 - dim))
    return level


def normal_values(stream_key, dims, spread, reach, shards=(), kind=jnp.bfloat16):
    array = jax.random.normal(stream_key, dims, jnp.float32) * spread
    if len(shards) > 0:
        array = block_scale(stream_key, dims, shards, -0.22, 0.18) * array
    return jnp.clip(array, min=-reach, max=reach).astype(kind)


def setup_inputs(seed: int = 0) -> dict:
    key_list = jax.random.split(jax.random.key(seed), 10)
    return {
        "events": normal_values(key_list[0], (EVENTS, D), 1.0, 6.0, ((0, 768),)),
        "user_ids": draw_user_ids(jax.random.fold_in(key_list[9], 71), 0),
        "session_break": place_ends((jax.random.randint(key_list[2], (EVENTS,), 0, 96) < 1).astype(jnp.int32), jax.random.fold_in(key_list[2], 1), 0, 1),
        "in_gain": jnp.clip(1.0 + 0.18 * jax.random.normal(key_list[3], (D,), jnp.float32), 0.1, 1.9),
        "in_weight": normal_values(key_list[4], (D, 2 * D), D ** -0.5, 0.1875),
        "decay_rates": draw_decay_rates(jax.random.fold_in(key_list[9], 71), 0),
        "keep_factor": jnp.clip(jax.random.uniform(key_list[6], (D,), jnp.float32, 0.4, 0.8), 0.4, 0.8),
        "out_gain": jnp.clip(1.0 + 0.18 * jax.random.normal(key_list[7], (D,), jnp.float32), 0.1, 1.9),
        "out_weight": normal_values(key_list[8], (D, D), D ** -0.5, 0.1875),
    }


def rms_scale(values, gain_vec):
    return values * lax.rsqrt(lax.optimization_barrier(jnp.mean(values * values, axis=-1, keepdims=True)) + 1e-06) * gain_vec

def reference(events, user_ids, session_break, in_gain, in_weight, decay_rates, keep_factor, out_gain, out_weight):
    event_rows = events.astype(jnp.float32)
    normed = rms_scale(event_rows, in_gain).astype(jnp.bfloat16)
    projected = jnp.dot(normed, in_weight, preferred_element_type=jnp.float32).astype(jnp.bfloat16)
    gate_part = projected[:, :D].astype(jnp.float32)
    base_decay = jnp.exp(-decay_rates)

    def advance(carry_state, step_item):
        user_now, break_now, value_now = step_item
        factor = base_decay * jnp.where(break_now == 1, keep_factor, jnp.ones_like(keep_factor))
        state_new = factor * carry_state[user_now] + value_now.astype(jnp.float32)
        return (carry_state.at[user_now].set(state_new), state_new)
    state_zero = jnp.zeros((USERS, D), decay_rates.dtype)
    _, hidden = lax.scan(advance, state_zero, (user_ids, session_break, projected[:, D:]))
    mixed_part = (rms_scale(hidden, out_gain) * jax.nn.silu(gate_part)).astype(jnp.bfloat16)
    return (event_rows + jnp.dot(mixed_part, out_weight, preferred_element_type=jnp.float32)).astype(jnp.bfloat16)
```

```python
import functools

import jax
import jax.numpy as jnp
from jax import lax
from jax.experimental import pallas as pl
from jax.experimental.pallas import tpu as pltpu
from jax.sharding import PartitionSpec as P

F32, BF16 = jnp.float32, jnp.bfloat16
MESH = pl.DeviceIdType.MESH
NZ = 12
NT = 8
LANES = 128
ROWS = 128
USERS = 192


def dot(a, b):
    return jnp.dot(a, b, preferred_element_type=F32)


def decay_of(counts, rate, log_keep):
    breaks = jnp.floor(counts * (1.0 / 16.0))
    return log_keep * breaks - rate * (counts - 16.0 * breaks)


def kernel(
    NC, NX, NY,
    ev_ref, ids_ref, brk_ref, in_gain_ref, rate_ref, keep_ref, out_gain_ref, w_in, w_out,
    out_ref,
    wv, wg, wo, vt, id_src, idb, vbuf, mt, mem, dcy, span, pre_q, pre_p,
    end_e, end_q, s1e, s1q, slab_e, slab_q, ye, yq, cst, cbuf, cacc,
    rsrc, rbuf, xloc, grow, sgate, acc, lk_ref,
    w_sem, id_send, id_recv, v_send, v_recv, q1_send, q1_recv, e1_send, e1_recv,
    yq_send, yq_recv, ye_send, ye_recv, c_send, c_recv, r_send, r_recv,
):
    NP = NC * NX
    UP = USERS // NP
    g, s = lax.axis_index("grp"), lax.axis_index("shard")
    y, c = lax.div(g, NC), lax.rem(g, NC)
    x, z = lax.div(s, NZ), lax.rem(s, NZ)
    line = c * NX + x
    zq, zr = lax.div(z, 3), lax.rem(z, 3)
    holder = zr < 2
    tile = zq + 4 * zr

    def at_z(zz):
        return (g, x * NZ + zz)

    def at_line(p):
        return (y * NC + p // NX, (p % NX) * NZ + z)

    def at_y(yy):
        return (yy * NC + c, s)

    def rcopy(src, dst, ss, rs, dev):
        return pltpu.make_async_remote_copy(
            src_ref=src, dst_ref=dst, send_sem=ss, recv_sem=rs, device_id=dev, device_id_type=MESH
        )

    half = NT * LANES // 2
    full = NT * LANES
    wcopies = [
        pltpu.make_async_copy(w_in.at[:, pl.ds(full, half)], wv.at[0], w_sem.at[0]),
        pltpu.make_async_copy(w_in.at[:, pl.ds(full + half, half)], wv.at[1], w_sem.at[1]),
        pltpu.make_async_copy(w_in.at[:, pl.ds(0, full)], wg, w_sem.at[2]),
        pltpu.make_async_copy(w_out, wo, w_sem.at[3]),
    ]
    for cp in wcopies:
        cp.start()

    barrier = pltpu.get_barrier_semaphore()
    for d in range(1, NZ):
        pl.semaphore_signal(barrier, inc=1, device_id=at_z(lax.rem(z + d, NZ)), device_id_type=MESH)

    @pl.when(holder)
    def _():
        for d in range(1, NP):
            p = lax.rem(line + d, NP)
            pl.semaphore_signal(barrier, inc=1, device_id=(y * NC + lax.div(p, NX), lax.rem(p, NX) * NZ + z), device_id_type=MESH)
        for d in range(1, NY):
            pl.semaphore_signal(barrier, inc=1, device_id=at_y(lax.rem(y + d, NY)), device_id_type=MESH)

    idr = ids_ref[...].astype(F32)
    brk = brk_ref[...].astype(F32)
    id_src[...] = jnp.concatenate([idr, brk, jnp.zeros((6, LANES), F32)], axis=0)
    lk_ref[...] = jnp.log(keep_ref[...])
    ev = ev_ref[...].astype(F32)
    mean = jnp.sum(ev * ev, axis=1, keepdims=True) * (1.0 / full)
    normed = (ev * lax.rsqrt(mean + 1e-6) * in_gain_ref[...]).astype(BF16)

    @pl.when(holder)
    def _():
        pl.semaphore_wait(barrier, NZ - 1 + NP - 1 + NY - 1)

    @pl.when(jnp.logical_not(holder))
    def _():
        pl.semaphore_wait(barrier, NZ - 1)

    def id_copy(t, zt):
        return rcopy(id_src, idb.at[z], id_send.at[t], id_recv.at[z], at_z(zt))

    def v_copy(t, zt):
        return rcopy(vt.at[t], vbuf.at[z], v_send.at[t], v_recv.at[z], at_z(zt))

    for t in range(NT):
        zt = 3 * (t % 4) + t // 4

        @pl.when(z == zt)
        def _():
            idb[z] = id_src[...]

        @pl.when(z != zt)
        def _():
            id_copy(t, zt).start()

    for grp in range(2):
        wcopies[grp].wait()
        v = dot(normed, wv[grp]).astype(BF16)
        for t in range(4):
            vt[4 * grp + t] = v[:, LANES * t : LANES * (t + 1)]
        for k in range(4):
            q = lax.rem(zq + k, 4)
            t, zt = q + 4 * grp, 3 * q + grp

            @pl.when(z == zt)
            def _():
                vbuf[z] = vt[t]

            @pl.when(z != zt)
            def _():
                v_copy(t, zt).start()

    sub = lax.broadcasted_iota(jnp.int32, (ROWS, LANES), 0)
    lane = lax.broadcasted_iota(jnp.int32, (ROWS, LANES), 1)
    ones = jnp.ones((LANES, LANES), BF16)

    @pl.when(holder)
    def _():
        at = pl.ds(pl.multiple_of(tile * LANES, LANES), LANES)
        rate, log_keep = rate_ref[:, at], lk_ref[:, at]
        ones2 = jnp.ones((LANES, 2 * LANES), BF16)
        lane2 = lax.broadcasted_iota(jnp.int32, (ROWS, 2 * LANES), 1).astype(F32)
        usub = lax.broadcasted_iota(jnp.int32, (USERS, LANES), 0).astype(F32)

        for zz in range(NZ):
            @pl.when(z != zz)
            def _():
                rcopy(id_src, idb.at[zz], id_send.at[0], id_recv.at[zz], at_z(zz)).wait_recv()

        pre_q[0] = jnp.ones((USERS, LANES), F32)

        def prep(zz, carry):
            info = idb[zz]
            row, weight = info[0:1], 1.0 + 16.0 * info[1:2]
            col = dot(jnp.where(sub == lane, row, 0.0).astype(BF16), ones2)
            mt[zz] = (col == lane2).astype(F32).astype(BF16)
            after = jnp.where((col[:, :LANES] == row) & (lane > sub), weight, 0.0).astype(BF16)
            dcy[zz] = jnp.exp(decay_of(dot(after, ones), rate, log_keep))
            own = usub == row
            mem[zz] = own.astype(F32).astype(BF16)
            sp = jnp.exp(decay_of(dot(jnp.where(own, weight, 0.0).astype(BF16), ones), rate, log_keep))
            span[zz] = sp
            pre_q[zz + 1] = pre_q[zz] * sp
            return carry

        lax.fori_loop(0, NZ, prep, 0)

        def q1_copy(p):
            return rcopy(end_q.at[p], s1q.at[line], q1_send.at[p], q1_recv.at[line], at_line(p))

        def e1_copy(p):
            return rcopy(end_e.at[p], s1e.at[line], e1_send.at[p], e1_recv.at[line], at_line(p))

        def c_copy(p):
            return rcopy(cst.at[p], cbuf.at[line], c_send.at[p], c_recv.at[line], at_line(p))

        def yq_copy(yy):
            return rcopy(slab_q, yq.at[y], yq_send.at[yy], yq_recv.at[y], at_y(yy))

        def ye_copy(yy):
            return rcopy(slab_e, ye.at[y], ye_send.at[yy], ye_recv.at[y], at_y(yy))

        def to_parts(src, dst, value, copy):
            for p in range(NP):
                part = value[UP * p : UP * (p + 1)]

                @pl.when(line == p)
                def _():
                    dst[p] = part

                @pl.when(line != p)
                def _():
                    src[p] = part
                    copy(p).start()

        def from_parts(src, dst, ss, rs):
            for p in range(NP):
                @pl.when(line != p)
                def _():
                    rcopy(src.at[p], dst.at[p], ss.at[p], rs.at[p], at_line(p)).wait_recv()

        to_parts(end_q, s1q, pre_q[NZ], q1_copy)
        from_parts(end_q, s1q, q1_send, q1_recv)
        q = s1q[0]
        for p in range(1, NP):
            q = q * s1q[p]
        slab_q[...] = q
        for yy in range(1, NY):
            @pl.when(yy > y)
            def _():
                yq_copy(yy).start()

        def ends(zz, p):
            @pl.when(z != zz)
            def _():
                rcopy(vt.at[0], vbuf.at[zz], v_send.at[0], v_recv.at[zz], at_z(zz)).wait_recv()

            w = dcy[zz] * vbuf[zz].astype(F32)
            hi = w.astype(BF16)
            lo = (w - hi.astype(F32)).astype(BF16)
            member = mem[zz]
            e = dot(member, hi) + dot(member, lo)
            pre_p[zz] = p
            return span[zz] * p + e

        total = lax.fori_loop(0, NZ, ends, jnp.zeros((USERS, LANES), F32))

        to_parts(end_e, s1e, total, e1_copy)
        from_parts(end_e, s1e, e1_send, e1_recv)
        e = s1e[0]
        for p in range(1, NP):
            e = s1q[p] * e + s1e[p]
        slab_e[...] = e
        for yy in range(1, NY):
            @pl.when(yy > y)
            def _():
                ye_copy(yy).start()

        cacc[...] = jnp.zeros((UP, LANES), F32)
        for yy in range(NY - 1):
            @pl.when(yy < y)
            def _():
                rcopy(slab_q, yq.at[yy], yq_send.at[yy], yq_recv.at[yy], at_y(yy)).wait_recv()
                rcopy(slab_e, ye.at[yy], ye_send.at[yy], ye_recv.at[yy], at_y(yy)).wait_recv()
                cacc[...] = yq[yy] * cacc[...] + ye[yy]

        start = cacc[...]
        for p in range(NP):
            @pl.when(line == p)
            def _():
                cbuf[p] = start

            @pl.when(line != p)
            def _():
                cst[p] = start
                c_copy(p).start()

            start = s1q[p] * start + s1e[p]
        from_parts(cst, cbuf, c_send, c_recv)

        def r_copy(zz):
            return rcopy(rsrc.at[zz], rbuf.at[tile], r_send.at[zz], r_recv.at[tile], at_z(zz))

        carry_in = jnp.concatenate([cbuf[p] for p in range(NP)], axis=0)
        pad = jnp.zeros((2 * LANES - USERS, LANES), BF16)

        def give(k, carry):
            zz = lax.rem(z + k + 6, NZ)
            states = (pre_p[zz] + pre_q[zz] * carry_in).astype(BF16)
            rsrc[zz] = dot(mt[zz], jnp.concatenate([states, pad], axis=0)).astype(BF16)

            @pl.when(zz == z)
            def _():
                rbuf[tile] = rsrc[zz]

            @pl.when(zz != z)
            def _():
                r_copy(zz).start()

            return carry

        lax.fori_loop(0, NZ, give, 0)

        for p in range(NP):
            @pl.when(line != p)
            def _():
                q1_copy(p).wait_send()
                e1_copy(p).wait_send()
                c_copy(p).wait_send()
        for yy in range(1, NY):
            @pl.when(yy > y)
            def _():
                yq_copy(yy).wait_send()
                ye_copy(yy).wait_send()

    wcopies[2].wait()
    weight = 1.0 + 16.0 * brk
    col = dot(jnp.where(sub == lane, idr, 0.0).astype(BF16), ones)
    upto = (col == idr) & (lane <= sub)
    counts = dot(jnp.where(upto, weight, 0.0).astype(BF16), ones)
    within = upto.astype(F32).astype(BF16)
    breaks = jnp.floor(counts * (1.0 / 16.0))
    events_of = counts - 16.0 * breaks
    for t in range(NT):
        cols = slice(LANES * t, LANES * (t + 1))
        level = lk_ref[:, cols] * breaks - rate_ref[:, cols] * events_of
        grow[t] = jnp.exp(level)
        scaled = jnp.exp(-level) * vt[t].astype(F32)
        hi = scaled.astype(BF16)
        lo = (scaled - hi.astype(F32)).astype(BF16)
        xloc[t] = dot(within, hi) + dot(within, lo)
    gate = dot(normed, wg[...]).astype(BF16).astype(F32)
    gate = out_gain_ref[...] * (gate / (1.0 + jnp.exp(-gate)))
    for t in range(NT):
        sgate[t] = gate[:, LANES * t : LANES * (t + 1)]

    wcopies[3].wait()
    squares = jnp.zeros((ROWS, LANES), F32)
    for t in range(0, NT, 2):
        parts = []
        for u in (t, t + 1):
            zt = 3 * (u % 4) + u // 4

            @pl.when(z != zt)
            def _():
                rcopy(rsrc.at[0], rbuf.at[u], r_send.at[0], r_recv.at[u], at_z(zt)).wait_recv()

            h = grow[u] * (xloc[u] + rbuf[u].astype(F32))
            squares = squares + h * h
            parts.append((h * sgate[u]).astype(BF16))
        prod = dot(jnp.concatenate(parts, axis=1), wo[LANES * t : LANES * (t + 2), :])
        if t == 0:
            acc[...] = prod
        else:
            acc[...] += prod
    mean_h = jnp.sum(squares, axis=1, keepdims=True) * (1.0 / full)
    out_ref[...] = (ev_ref[...].astype(F32) + acc[...] * lax.rsqrt(mean_h + 1e-6)).astype(BF16)

    for t in range(NT):
        zt = 3 * (t % 4) + t // 4

        @pl.when(z != zt)
        def _():
            id_copy(t, zt).wait_send()
            v_copy(t, zt).wait_send()

    @pl.when(holder)
    def _():
        for zz in range(NZ):
            @pl.when(z != zz)
            def _():
                rcopy(rsrc.at[zz], rbuf.at[tile], r_send.at[zz], r_recv.at[tile], at_z(zz)).wait_send()


def on_device(NC, NX, NY, events, user_ids, session_break, in_gain, in_weight, decay_rates, keep_factor, out_gain, out_weight):
    NP = NC * NX
    UP = USERS // NP
    D = NT * LANES
    vmem = pl.BlockSpec(memory_space=pltpu.VMEM)
    hbm = pl.BlockSpec(memory_space=pl.ANY)
    V = pltpu.VMEM
    dma = lambda *n: pltpu.SemaphoreType.DMA(n)
    return pl.pallas_call(
        functools.partial(kernel, NC, NX, NY),
        out_shape=jax.ShapeDtypeStruct((ROWS, D), BF16),
        in_specs=[vmem] * 7 + [hbm] * 2,
        out_specs=vmem,
        scratch_shapes=[
            V((2, D, D // 2), BF16), V((D, D), BF16), V((D, D), BF16),
            V((NT, ROWS, LANES), BF16), V((8, LANES), F32), V((NZ, 8, LANES), F32),
            V((NZ, ROWS, LANES), BF16), V((NZ, ROWS, 2 * LANES), BF16), V((NZ, USERS, LANES), BF16),
            V((NZ, ROWS, LANES), F32), V((NZ, USERS, LANES), F32), V((NZ + 1, USERS, LANES), F32),
            V((NZ, USERS, LANES), F32),
            V((NP, UP, LANES), F32), V((NP, UP, LANES), F32), V((NP, UP, LANES), F32), V((NP, UP, LANES), F32),
            V((UP, LANES), F32), V((UP, LANES), F32), V((NY, UP, LANES), F32), V((NY, UP, LANES), F32),
            V((NP, UP, LANES), F32), V((NP, UP, LANES), F32), V((UP, LANES), F32),
            V((NZ, ROWS, LANES), BF16), V((NT, ROWS, LANES), BF16),
            V((NT, ROWS, LANES), F32), V((NT, ROWS, LANES), F32), V((NT, ROWS, LANES), F32),
            V((ROWS, D), F32), V((1, D), F32),
            dma(4), dma(NT), dma(NZ), dma(NT), dma(NZ), dma(NP), dma(NP), dma(NP), dma(NP),
            dma(NY), dma(NY), dma(NY), dma(NY), dma(NP), dma(NP), dma(NZ), dma(NT),
        ],
        compiler_params=pltpu.CompilerParams(
            collective_id=0, has_side_effects=True, vmem_limit_bytes=48 * 1024 * 1024
        ),
    )(
        events, user_ids.reshape(1, ROWS), session_break.reshape(1, ROWS),
        in_gain.reshape(1, D), decay_rates.reshape(1, D), keep_factor.reshape(1, D),
        out_gain.reshape(1, D), in_weight, out_weight,
    )


def solution(mesh):
    groups, shards = mesh.shape["grp"], mesh.shape["shard"]
    NC = 2 if groups % 2 == 0 else 1
    body = functools.partial(on_device, NC, shards // NZ, groups // NC)
    both = P(("grp", "shard"))
    return jax.shard_map(
        body,
        mesh=mesh,
        in_specs=(P(("grp", "shard"), None), both, both, P(), P(), P(), P(), P(), P()),
        out_specs=P(("grp", "shard"), None),
        check_vma=False,
    )
```

```python
import functools

import jax
import jax.numpy as jnp
from jax import lax
from jax.experimental import pallas as pl
from jax.experimental.pallas import tpu as pltpu
from jax.sharding import PartitionSpec as P

F32, BF16 = jnp.float32, jnp.bfloat16
MESH = pl.DeviceIdType.MESH
NZ = 12
NT = 8
LANES = 128
ROWS = 128
USERS = 192
GROUP = 4


def dot(a, b):
    return jnp.dot(a, b, preferred_element_type=F32)


def decay_of(counts, rate, log_keep):
    breaks = jnp.floor(counts * (1.0 / 16.0))
    return log_keep * breaks - rate * (counts - 16.0 * breaks)


def kernel(
    NC, NX, NY,
    ev_hbm, ids_hbm, brk_hbm, in_gain_hbm, rate_hbm, keep_hbm, out_gain_hbm, w_in, w_out,
    out_ref,
    ev_ref, ids_ref, brk_ref, in_gain_ref, rate_ref, keep_ref, out_gain_ref,
    wv, wg, wo, vt, id_src, idb, vbuf, mt, mem, dcy, span, pre_q, pre_p, end,
    end_e, end_q, s1e, s1q, slab_e, slab_q, ye, yq, cst, cbuf, cacc,
    rsrc, rbuf, xloc, grow, sgate, acc, lk_ref,
    op_sem, w_sem, id_send, id_recv, v_send, v_recv, q1_send, q1_recv, e1_send, e1_recv,
    yq_send, yq_recv, ye_send, ye_recv, c_send, c_recv, r_send, r_recv, ready,
):
    NP = NC * NX
    UP = USERS // NP
    g, s = lax.axis_index("grp"), lax.axis_index("shard")
    y, c = lax.div(g, NC), lax.rem(g, NC)
    x, z = lax.div(s, NZ), lax.rem(s, NZ)
    line = c * NX + x
    zq, zr = lax.div(z, 3), lax.rem(z, 3)
    holder = zr < 2
    tile = 2 * zq + zr

    def at_z(zz):
        return (g, x * NZ + zz)

    def at_line(p):
        return (y * NC + p // NX, (p % NX) * NZ + z)

    def at_y(yy):
        return (yy * NC + c, s)

    def rcopy(src, dst, ss, rs, dev):
        return pltpu.make_async_remote_copy(
            src_ref=src, dst_ref=dst, send_sem=ss, recv_sem=rs, device_id=dev, device_id_type=MESH
        )

    ocopies = [
        pltpu.make_async_copy(src, dst, op_sem.at[i])
        for i, (src, dst) in enumerate((
            (ids_hbm, ids_ref), (brk_hbm, brk_ref), (ev_hbm, ev_ref), (in_gain_hbm, in_gain_ref),
            (rate_hbm, rate_ref), (keep_hbm, keep_ref), (out_gain_hbm, out_gain_ref),
        ))
    ]
    for cp in ocopies:
        cp.start()
    half = NT * LANES // 2
    full = NT * LANES
    wcopies = [
        pltpu.make_async_copy(w_in.at[:, pl.ds(full, half)], wv.at[0], w_sem.at[0]),
        pltpu.make_async_copy(w_in.at[:, pl.ds(full + half, half)], wv.at[1], w_sem.at[1]),
        pltpu.make_async_copy(w_in.at[:, pl.ds(0, full)], wg, w_sem.at[2]),
        pltpu.make_async_copy(w_out, wo, w_sem.at[3]),
    ]
    for cp in wcopies[:2]:
        cp.start()

    barrier = pltpu.get_barrier_semaphore()
    for zz in range(1, NZ):
        @pl.when(z < zz)
        def _():
            pl.semaphore_signal(barrier, inc=1, device_id=at_z(zz), device_id_type=MESH)

    @pl.when(holder)
    def _():
        for d in range(1, NP):
            p = lax.rem(line + d, NP)
            pl.semaphore_signal(barrier, inc=1, device_id=(y * NC + lax.div(p, NX), lax.rem(p, NX) * NZ + z), device_id_type=MESH)
        for d in range(1, NY):
            pl.semaphore_signal(barrier, inc=1, device_id=at_y(lax.rem(y + d, NY)), device_id_type=MESH)

    for cp in ocopies[:2]:
        cp.wait()
    idr = ids_ref[...].astype(F32)
    brk = brk_ref[...].astype(F32)
    id_src[...] = jnp.concatenate([idr, brk, jnp.zeros((6, LANES), F32)], axis=0)

    @pl.when(holder)
    def _():
        pl.semaphore_wait(barrier, z + NP - 1 + NY - 1)

    @pl.when(jnp.logical_not(holder))
    def _():
        pl.semaphore_wait(barrier, z)

    for zz in range(NZ - 1):
        @pl.when((z > zz) & (holder if zz % 3 == 2 else z > zz))
        def _():
            pl.semaphore_signal(ready.at[z], inc=1, device_id=at_z(zz), device_id_type=MESH)

    def id_copy(t, zt):
        return rcopy(id_src, idb.at[z], id_send.at[t], id_recv.at[z], at_z(zt))

    def v_copy(t, zt):
        return rcopy(vt.at[t], vbuf.at[z], v_send.at[t], v_recv.at[z], at_z(zt))

    for t in range(NT):
        zt = 3 * (t // 2) + t % 2

        @pl.when(z == zt)
        def _():
            idb[z] = id_src[...]

        @pl.when(z > zt)
        def _():
            id_copy(t, zt).start()

    for cp in ocopies[2:]:
        cp.wait()
    lk_ref[...] = jnp.log(keep_ref[...])
    ev = ev_ref[...].astype(F32)
    mean = jnp.sum(ev * ev, axis=1, keepdims=True) * (1.0 / full)
    normed = (ev * lax.rsqrt(mean + 1e-6) * in_gain_ref[...]).astype(BF16)
    for grp in range(2):
        wcopies[grp].wait()
        if grp == 1:
            for cp in wcopies[2:]:
                cp.start()
        v = dot(normed, wv[grp]).astype(BF16)
        for t in range(4):
            vt[4 * grp + t] = v[:, LANES * t : LANES * (t + 1)]

    for t in range(NT):
        zt = 3 * (t // 2) + t % 2

        @pl.when(z < zt)
        def _():
            pl.semaphore_wait(ready.at[zt], 1)
            id_copy(t, zt).start()

        @pl.when(z == zt)
        def _():
            vbuf[z] = vt[t]

        @pl.when(z != zt)
        def _():
            v_copy(t, zt).start()

    sub = lax.broadcasted_iota(jnp.int32, (ROWS, LANES), 0)
    lane = lax.broadcasted_iota(jnp.int32, (ROWS, LANES), 1)
    ones = jnp.ones((LANES, LANES), BF16)

    wcopies[2].wait()
    weight = 1.0 + 16.0 * brk
    col = dot(jnp.where(sub == lane, idr, 0.0).astype(BF16), ones)
    upto = (col == idr) & (lane <= sub)
    counts = dot(jnp.where(upto, weight, 0.0).astype(BF16), ones)
    within = upto.astype(F32).astype(BF16)
    within = jnp.concatenate([within, within], axis=1)
    breaks = jnp.floor(counts * (1.0 / 16.0))
    events_of = counts - 16.0 * breaks
    for t in range(NT):
        cols = slice(LANES * t, LANES * (t + 1))
        level = lk_ref[:, cols] * breaks - rate_ref[:, cols] * events_of
        grow[t] = jnp.exp(level)
        scaled = jnp.exp(-level) * vt[t].astype(F32)
        hi = scaled.astype(BF16)
        lo = (scaled - hi.astype(F32)).astype(BF16)
        xloc[t] = dot(within, jnp.concatenate([hi, lo], axis=0))
    gate = dot(normed, wg[...]).astype(BF16).astype(F32)
    gate = out_gain_ref[...] * (gate / (1.0 + jnp.exp(-gate)))
    for t in range(NT):
        sgate[t] = gate[:, LANES * t : LANES * (t + 1)]

    @pl.when(holder)
    def _():
        at = pl.ds(pl.multiple_of(tile * LANES, LANES), LANES)
        rate, log_keep = rate_ref[:, at], lk_ref[:, at]
        ones2 = jnp.ones((LANES, 2 * LANES), BF16)
        lane2 = lax.broadcasted_iota(jnp.int32, (ROWS, 2 * LANES), 1).astype(F32)
        usub = lax.broadcasted_iota(jnp.int32, (USERS, LANES), 0).astype(F32)

        pre_q[0] = jnp.ones((USERS, LANES), F32)

        def prep(zz):
            info = idb[zz]
            row, weight = info[0:1], 1.0 + 16.0 * info[1:2]
            col = dot(jnp.where(sub == lane, row, 0.0).astype(BF16), ones2)
            mt[zz] = (col == lane2).astype(F32).astype(BF16)
            after = jnp.where((col[:, :LANES] == row) & (lane > sub), weight, 0.0).astype(BF16)
            dcy[zz] = jnp.exp(decay_of(dot(after, ones), rate, log_keep))
            own = usub == row
            own_b = own.astype(F32).astype(BF16)
            mem[zz] = jnp.concatenate([own_b, own_b], axis=1)
            sp = jnp.exp(decay_of(dot(jnp.where(own, weight, 0.0).astype(BF16), ones), rate, log_keep))
            span[zz] = sp
            pre_q[zz + 1] = pre_q[zz] * sp

        def prep_some(i, carry):
            for j in range(GROUP):
                zz = i * GROUP + j

                @pl.when(z != zz)
                def _():
                    rcopy(id_src, idb.at[zz], id_send.at[0], id_recv.at[zz], at_z(zz)).wait_recv()

            for j in range(GROUP):
                prep(i * GROUP + j)
            return carry

        lax.fori_loop(0, NZ // GROUP, prep_some, 0)

        def q1_copy(p):
            return rcopy(end_q.at[p], s1q.at[line], q1_send.at[p], q1_recv.at[line], at_line(p))

        def e1_copy(p):
            return rcopy(end_e.at[p], s1e.at[line], e1_send.at[p], e1_recv.at[line], at_line(p))

        def c_copy(p):
            return rcopy(cst.at[p], cbuf.at[line], c_send.at[p], c_recv.at[line], at_line(p))

        def yq_copy(yy):
            return rcopy(slab_q, yq.at[y], yq_send.at[yy], yq_recv.at[y], at_y(yy))

        def ye_copy(yy):
            return rcopy(slab_e, ye.at[y], ye_send.at[yy], ye_recv.at[y], at_y(yy))

        def to_parts(src, dst, value, copy):
            for p in range(NP):
                part = value[UP * p : UP * (p + 1)]

                @pl.when(line == p)
                def _():
                    dst[p] = part

                @pl.when(line != p)
                def _():
                    src[p] = part
                    copy(p).start()

        def from_parts(src, dst, ss, rs):
            for p in range(NP):
                @pl.when(line != p)
                def _():
                    rcopy(src.at[p], dst.at[p], ss.at[p], rs.at[p], at_line(p)).wait_recv()

        to_parts(end_q, s1q, pre_q[NZ], q1_copy)

        def spans_on():
            from_parts(end_q, s1q, q1_send, q1_recv)
            q = s1q[0]
            for p in range(1, NP):
                q = q * s1q[p]
            slab_q[...] = q
            for yy in range(1, NY):
                @pl.when(yy > y)
                def _():
                    yq_copy(yy).start()

        def ends(zz):
            w = dcy[zz] * vbuf[zz].astype(F32)
            hi = w.astype(BF16)
            lo = (w - hi.astype(F32)).astype(BF16)
            end[zz] = dot(mem[zz], jnp.concatenate([hi, lo], axis=0))

        total = jnp.zeros((USERS, LANES), F32)
        for i in range(0, NZ, GROUP):
            if i + GROUP == NZ:
                spans_on()
            for zz in range(i, i + GROUP):
                @pl.when(z != zz)
                def _():
                    rcopy(vt.at[0], vbuf.at[zz], v_send.at[0], v_recv.at[zz], at_z(zz)).wait_recv()

            for zz in range(i, i + GROUP):
                ends(zz)
            for zz in range(i, i + GROUP):
                pre_p[zz] = total
                total = span[zz] * total + end[zz]

        to_parts(end_e, s1e, total, e1_copy)
        from_parts(end_e, s1e, e1_send, e1_recv)
        e = s1e[0]
        for p in range(1, NP):
            e = s1q[p] * e + s1e[p]
        slab_e[...] = e
        for yy in range(1, NY):
            @pl.when(yy > y)
            def _():
                ye_copy(yy).start()

        cacc[...] = jnp.zeros((UP, LANES), F32)
        for yy in range(NY - 1):
            @pl.when(yy < y)
            def _():
                rcopy(slab_q, yq.at[yy], yq_send.at[yy], yq_recv.at[yy], at_y(yy)).wait_recv()
                rcopy(slab_e, ye.at[yy], ye_send.at[yy], ye_recv.at[yy], at_y(yy)).wait_recv()
                cacc[...] = yq[yy] * cacc[...] + ye[yy]

        start = cacc[...]
        for p in range(NP):
            @pl.when(line == p)
            def _():
                cbuf[p] = start

            @pl.when(line != p)
            def _():
                cst[p] = start
                c_copy(p).start()

            start = s1q[p] * start + s1e[p]
        from_parts(cst, cbuf, c_send, c_recv)

        def r_copy(zz):
            return rcopy(rsrc.at[zz], rbuf.at[tile], r_send.at[zz], r_recv.at[tile], at_z(zz))

        carry_in = jnp.concatenate([cbuf[p] for p in range(NP)], axis=0)
        pad = jnp.zeros((2 * LANES - USERS, LANES), BF16)

        def give(i, carry):
            blocks = [i * GROUP + j for j in range(GROUP)]
            for zz in blocks:
                states = (pre_p[zz] + pre_q[zz] * carry_in).astype(BF16)
                rsrc[zz] = dot(mt[zz], jnp.concatenate([states, pad], axis=0)).astype(BF16)
            for zz in blocks:
                @pl.when(zz == z)
                def _():
                    rbuf[tile] = rsrc[zz]

                @pl.when((zz > z) & (lax.rem(zz, 3) == 2))
                def _():
                    pl.semaphore_wait(ready.at[zz], 1)

                @pl.when(zz != z)
                def _():
                    r_copy(zz).start()

            return carry

        lax.fori_loop(0, NZ // GROUP, give, 0)

        for p in range(NP):
            @pl.when(line != p)
            def _():
                q1_copy(p).wait_send()
                e1_copy(p).wait_send()
                c_copy(p).wait_send()
        for yy in range(1, NY):
            @pl.when(yy > y)
            def _():
                yq_copy(yy).wait_send()
                ye_copy(yy).wait_send()

    wcopies[3].wait()
    squares = jnp.zeros((ROWS, LANES), F32)
    for t in range(0, NT, 2):
        parts = []
        for u in (t, t + 1):
            zt = 3 * (u // 2) + u % 2

            @pl.when(z != zt)
            def _():
                rcopy(rsrc.at[0], rbuf.at[u], r_send.at[0], r_recv.at[u], at_z(zt)).wait_recv()

            h = grow[u] * (xloc[u] + rbuf[u].astype(F32))
            squares = squares + h * h
            parts.append((h * sgate[u]).astype(BF16))
        prod = dot(jnp.concatenate(parts, axis=1), wo[LANES * t : LANES * (t + 2), :])
        if t == 0:
            acc[...] = prod
        else:
            acc[...] += prod
    mean_h = jnp.sum(squares, axis=1, keepdims=True) * (1.0 / full)
    out_ref[...] = (ev_ref[...].astype(F32) + acc[...] * lax.rsqrt(mean_h + 1e-6)).astype(BF16)

    for t in range(NT):
        zt = 3 * (t // 2) + t % 2

        @pl.when(z != zt)
        def _():
            id_copy(t, zt).wait_send()
            v_copy(t, zt).wait_send()

    @pl.when(holder)
    def _():
        for zz in range(NZ):
            @pl.when(z != zz)
            def _():
                rcopy(rsrc.at[zz], rbuf.at[tile], r_send.at[zz], r_recv.at[tile], at_z(zz)).wait_send()


def on_device(NC, NX, NY, events, user_ids, session_break, in_gain, in_weight, decay_rates, keep_factor, out_gain, out_weight):
    NP = NC * NX
    UP = USERS // NP
    D = NT * LANES
    vmem = pl.BlockSpec(memory_space=pltpu.VMEM)
    hbm = pl.BlockSpec(memory_space=pl.ANY)
    V = pltpu.VMEM
    dma = lambda *n: pltpu.SemaphoreType.DMA(n)
    return pl.pallas_call(
        functools.partial(kernel, NC, NX, NY),
        out_shape=jax.ShapeDtypeStruct((ROWS, D), BF16),
        in_specs=[hbm] * 9,
        out_specs=vmem,
        scratch_shapes=[
            V((ROWS, D), BF16), V((1, ROWS), jnp.int32), V((1, ROWS), jnp.int32),
            V((1, D), F32), V((1, D), F32), V((1, D), F32), V((1, D), F32),
            V((2, D, D // 2), BF16), V((D, D), BF16), V((D, D), BF16),
            V((NT, ROWS, LANES), BF16), V((8, LANES), F32), V((NZ, 8, LANES), F32),
            V((NZ, ROWS, LANES), BF16), V((NZ, ROWS, 2 * LANES), BF16), V((NZ, USERS, 2 * LANES), BF16),
            V((NZ, ROWS, LANES), F32), V((NZ, USERS, LANES), F32), V((NZ + 1, USERS, LANES), F32),
            V((NZ, USERS, LANES), F32), V((NZ, USERS, LANES), F32),
            V((NP, UP, LANES), F32), V((NP, UP, LANES), F32), V((NP, UP, LANES), F32), V((NP, UP, LANES), F32),
            V((UP, LANES), F32), V((UP, LANES), F32), V((NY, UP, LANES), F32), V((NY, UP, LANES), F32),
            V((NP, UP, LANES), F32), V((NP, UP, LANES), F32), V((UP, LANES), F32),
            V((NZ, ROWS, LANES), BF16), V((NT, ROWS, LANES), BF16),
            V((NT, ROWS, LANES), F32), V((NT, ROWS, LANES), F32), V((NT, ROWS, LANES), F32),
            V((ROWS, D), F32), V((1, D), F32),
            dma(7), dma(4), dma(NT), dma(NZ), dma(NT), dma(NZ), dma(NP), dma(NP), dma(NP), dma(NP),
            dma(NY), dma(NY), dma(NY), dma(NY), dma(NP), dma(NP), dma(NZ), dma(NT),
            pltpu.SemaphoreType.REGULAR((NZ,)),
        ],
        compiler_params=pltpu.CompilerParams(
            collective_id=0, has_side_effects=True, vmem_limit_bytes=60 * 1024 * 1024
        ),
    )(
        events, user_ids.reshape(1, ROWS), session_break.reshape(1, ROWS),
        in_gain.reshape(1, D), decay_rates.reshape(1, D), keep_factor.reshape(1, D),
        out_gain.reshape(1, D), in_weight, out_weight,
    )


def solution(mesh):
    groups, shards = mesh.shape["grp"], mesh.shape["shard"]
    NC = 2 if groups % 2 == 0 else 1
    body = functools.partial(on_device, NC, shards // NZ, groups // NC)
    both = P(("grp", "shard"))
    return jax.shard_map(
        body,
        mesh=mesh,
        in_specs=(P(("grp", "shard"), None), both, both, P(), P(), P(), P(), P(), P()),
        out_specs=P(("grp", "shard"), None),
        check_vma=False,
    )
```

```python
import functools

import jax
import jax.numpy as jnp
from jax import lax
from jax.experimental import pallas as pl
from jax.experimental.pallas import tpu as pltpu
from jax.sharding import PartitionSpec as P

F32, BF16 = jnp.float32, jnp.bfloat16
MESH = pl.DeviceIdType.MESH
NZ = 12
NT = 8
LANES = 128
ROWS = 128
USERS = 192
GROUP = 4


def dot(a, b):
    return jnp.dot(a, b, preferred_element_type=F32)


def decay_of(counts, rate, log_keep):
    breaks = jnp.floor(counts * (1.0 / 16.0))
    return log_keep * breaks - rate * (counts - 16.0 * breaks)


def kernel(
    NC, NX, NY,
    ev_hbm, ids_hbm, brk_hbm, in_gain_hbm, rate_hbm, keep_hbm, out_gain_hbm, w_in, w_out,
    out_ref,
    ev_ref, ids_ref, brk_ref, in_gain_ref, rate_ref, keep_ref, out_gain_ref,
    wv, wg, wo, vt, id_src, idb, vbuf, mt, mem, dcy, span, pre_q, pre_p, end,
    end_e, end_q, s1e, s1q, slab_e, slab_q, ye, yq, cst, cbuf, cacc,
    rsrc, rbuf, xloc, grow, sgate, acc, lk_ref,
    op_sem, w_sem, id_send, id_recv, v_send, v_recv, q1_send, q1_recv, e1_send, e1_recv,
    yq_send, yq_recv, ye_send, ye_recv, c_send, c_recv, r_send, r_recv, ready, lines, go,
):
    NP = NC * NX
    UP = USERS // NP
    g, s = lax.axis_index("grp"), lax.axis_index("shard")
    y, c = lax.div(g, NC), lax.rem(g, NC)
    x, z = lax.div(s, NZ), lax.rem(s, NZ)
    line = c * NX + x
    holder = (lax.rem(z, 4) < 3) & (z < 10)
    tile = z - lax.div(z, 4)

    def at_z(zz):
        return (g, x * NZ + zz)

    def at_line(p):
        return (y * NC + p // NX, (p % NX) * NZ + z)

    def at_y(yy):
        return (yy * NC + c, s)

    def rcopy(src, dst, ss, rs, dev):
        return pltpu.make_async_remote_copy(
            src_ref=src, dst_ref=dst, send_sem=ss, recv_sem=rs, device_id=dev, device_id_type=MESH
        )

    ocopies = [
        pltpu.make_async_copy(src, dst, op_sem.at[i])
        for i, (src, dst) in enumerate((
            (ids_hbm, ids_ref), (brk_hbm, brk_ref), (ev_hbm, ev_ref), (in_gain_hbm, in_gain_ref),
            (rate_hbm, rate_ref), (keep_hbm, keep_ref), (out_gain_hbm, out_gain_ref),
        ))
    ]
    for cp in ocopies:
        cp.start()
    half = NT * LANES // 2
    full = NT * LANES
    wcopies = [
        pltpu.make_async_copy(w_in.at[:, pl.ds(full, half)], wv.at[0], w_sem.at[0]),
        pltpu.make_async_copy(w_in.at[:, pl.ds(full + half, half)], wv.at[1], w_sem.at[1]),
        pltpu.make_async_copy(w_in.at[:, pl.ds(0, full)], wg, w_sem.at[2]),
        pltpu.make_async_copy(w_out, wo, w_sem.at[3]),
    ]
    for cp in wcopies[:2]:
        cp.start()

    barrier = pltpu.get_barrier_semaphore()
    for zz in range(1, NZ):
        @pl.when(z < zz)
        def _():
            pl.semaphore_signal(barrier, inc=1, device_id=at_z(zz), device_id_type=MESH)

    def tell_peers(sem):
        for d in range(1, NP):
            p = lax.rem(line + d, NP)
            peer = (y * NC + lax.div(p, NX), lax.rem(p, NX) * NZ + z)
            pl.semaphore_signal(sem, inc=1, device_id=peer, device_id_type=MESH)
        for d in range(1, NY):
            pl.semaphore_signal(sem, inc=1, device_id=at_y(lax.rem(y + d, NY)), device_id_type=MESH)

    peers = NP - 1 + NY - 1

    @pl.when(z == 0)
    def _():
        tell_peers(barrier)

    for cp in ocopies[:2]:
        cp.wait()
    idr = ids_ref[...].astype(F32)
    brk = brk_ref[...].astype(F32)
    id_src[...] = jnp.concatenate([idr, brk, jnp.zeros((6, LANES), F32)], axis=0)

    @pl.when(z == 0)
    def _():
        pl.semaphore_wait(barrier, peers)

    @pl.when(z > 0)
    def _():
        pl.semaphore_wait(barrier, z)

    for zz in range(NZ - 1):
        @pl.when((z > zz) & (z > zz if zz % 4 < 3 and zz < 10 else holder))
        def _():
            pl.semaphore_signal(ready.at[z], inc=1, device_id=at_z(zz), device_id_type=MESH)

    def id_copy(t, zt):
        return rcopy(id_src, idb.at[z], id_send.at[t], id_recv.at[z], at_z(zt))

    def v_copy(t, zt):
        return rcopy(vt.at[t], vbuf.at[z], v_send.at[t], v_recv.at[z], at_z(zt))

    for t in range(NT):
        zt = t + t // 3

        @pl.when(z == zt)
        def _():
            idb[z] = id_src[...]

        @pl.when(z > zt)
        def _():
            id_copy(t, zt).start()

    for cp in ocopies[2:]:
        cp.wait()
    lk_ref[...] = jnp.log(keep_ref[...])
    ev = ev_ref[...].astype(F32)
    mean = jnp.sum(ev * ev, axis=1, keepdims=True) * (1.0 / full)
    normed = (ev * lax.rsqrt(mean + 1e-6) * in_gain_ref[...]).astype(BF16)
    for grp in range(2):
        wcopies[grp].wait()
        if grp == 1:
            for cp in wcopies[2:]:
                cp.start()
        v = dot(normed, wv[grp]).astype(BF16)
        for t in range(4):
            vt[4 * grp + t] = v[:, LANES * t : LANES * (t + 1)]

    for t in range(NT):
        zt = t + t // 3

        @pl.when(z < zt)
        def _():
            pl.semaphore_wait(ready.at[zt], 1)
            id_copy(t, zt).start()

        @pl.when(z == zt)
        def _():
            vbuf[z] = vt[t]

        @pl.when(z != zt)
        def _():
            v_copy(t, zt).start()

    @pl.when(z == 0)
    def _():
        tell_peers(lines)

    sub = lax.broadcasted_iota(jnp.int32, (ROWS, LANES), 0)
    lane = lax.broadcasted_iota(jnp.int32, (ROWS, LANES), 1)
    ones = jnp.ones((LANES, LANES), BF16)

    wcopies[2].wait()
    weight = 1.0 + 16.0 * brk
    col = dot(jnp.where(sub == lane, idr, 0.0).astype(BF16), ones)
    upto = (col == idr) & (lane <= sub)
    counts = dot(jnp.where(upto, weight, 0.0).astype(BF16), ones)
    within = upto.astype(F32).astype(BF16)
    within = jnp.concatenate([within, within], axis=1)
    breaks = jnp.floor(counts * (1.0 / 16.0))
    events_of = counts - 16.0 * breaks
    for t in range(NT):
        cols = slice(LANES * t, LANES * (t + 1))
        level = lk_ref[:, cols] * breaks - rate_ref[:, cols] * events_of
        grow[t] = jnp.exp(level)
        scaled = jnp.exp(-level) * vt[t].astype(F32)
        hi = scaled.astype(BF16)
        lo = (scaled - hi.astype(F32)).astype(BF16)
        xloc[t] = dot(within, jnp.concatenate([hi, lo], axis=0))
    gate = dot(normed, wg[...]).astype(BF16).astype(F32)
    gate = out_gain_ref[...] * (gate / (1.0 + jnp.exp(-gate)))
    for t in range(NT):
        sgate[t] = gate[:, LANES * t : LANES * (t + 1)]

    @pl.when(z == 0)
    def _():
        pl.semaphore_wait(lines, peers)
        for t in range(1, NT):
            pl.semaphore_signal(go, inc=1, device_id=at_z(t + t // 3), device_id_type=MESH)

    @pl.when(holder)
    def _():
        at = pl.ds(pl.multiple_of(tile * LANES, LANES), LANES)
        rate, log_keep = rate_ref[:, at], lk_ref[:, at]
        ones2 = jnp.ones((LANES, 2 * LANES), BF16)
        lane2 = lax.broadcasted_iota(jnp.int32, (ROWS, 2 * LANES), 1).astype(F32)
        usub = lax.broadcasted_iota(jnp.int32, (USERS, LANES), 0).astype(F32)

        pre_q[0] = jnp.ones((USERS, LANES), F32)

        def prep(zz):
            info = idb[zz]
            row, weight = info[0:1], 1.0 + 16.0 * info[1:2]
            col = dot(jnp.where(sub == lane, row, 0.0).astype(BF16), ones2)
            mt[zz] = (col == lane2).astype(F32).astype(BF16)
            after = jnp.where((col[:, :LANES] == row) & (lane > sub), weight, 0.0).astype(BF16)
            dcy[zz] = jnp.exp(decay_of(dot(after, ones), rate, log_keep))
            own = usub == row
            own_b = own.astype(F32).astype(BF16)
            mem[zz] = jnp.concatenate([own_b, own_b], axis=1)
            sp = jnp.exp(decay_of(dot(jnp.where(own, weight, 0.0).astype(BF16), ones), rate, log_keep))
            span[zz] = sp
            pre_q[zz + 1] = pre_q[zz] * sp

        def prep_some(i, carry):
            for j in range(GROUP):
                zz = i * GROUP + j

                @pl.when(z != zz)
                def _():
                    rcopy(id_src, idb.at[zz], id_send.at[0], id_recv.at[zz], at_z(zz)).wait_recv()

            for j in range(GROUP):
                prep(i * GROUP + j)
            return carry

        lax.fori_loop(0, NZ // GROUP, prep_some, 0)

        def q1_copy(p):
            return rcopy(end_q.at[p], s1q.at[line], q1_send.at[p], q1_recv.at[line], at_line(p))

        def e1_copy(p):
            return rcopy(end_e.at[p], s1e.at[line], e1_send.at[p], e1_recv.at[line], at_line(p))

        def c_copy(p):
            return rcopy(cst.at[p], cbuf.at[line], c_send.at[p], c_recv.at[line], at_line(p))

        def yq_copy(yy):
            return rcopy(slab_q, yq.at[y], yq_send.at[yy], yq_recv.at[y], at_y(yy))

        def ye_copy(yy):
            return rcopy(slab_e, ye.at[y], ye_send.at[yy], ye_recv.at[y], at_y(yy))

        def to_parts(src, dst, value, copy):
            for p in range(NP):
                part = value[UP * p : UP * (p + 1)]

                @pl.when(line == p)
                def _():
                    dst[p] = part

                @pl.when(line != p)
                def _():
                    src[p] = part
                    copy(p).start()

        def from_parts(src, dst, ss, rs):
            for p in range(NP):
                @pl.when(line != p)
                def _():
                    rcopy(src.at[p], dst.at[p], ss.at[p], rs.at[p], at_line(p)).wait_recv()

        def spans_on():
            from_parts(end_q, s1q, q1_send, q1_recv)
            q = s1q[0]
            for p in range(1, NP):
                q = q * s1q[p]
            slab_q[...] = q
            for yy in range(1, NY):
                @pl.when(yy > y)
                def _():
                    yq_copy(yy).start()

        def ends(zz):
            w = dcy[zz] * vbuf[zz].astype(F32)
            hi = w.astype(BF16)
            lo = (w - hi.astype(F32)).astype(BF16)
            end[zz] = dot(mem[zz], jnp.concatenate([hi, lo], axis=0))

        total = jnp.zeros((USERS, LANES), F32)
        for i in range(0, NZ, GROUP):
            if i + GROUP == NZ:
                @pl.when(z > 0)
                def _():
                    pl.semaphore_wait(go, 1)

                to_parts(end_q, s1q, pre_q[NZ], q1_copy)
            for zz in range(i, i + GROUP):
                @pl.when(z != zz)
                def _():
                    rcopy(vt.at[0], vbuf.at[zz], v_send.at[0], v_recv.at[zz], at_z(zz)).wait_recv()

            for zz in range(i, i + GROUP):
                ends(zz)
            for zz in range(i, i + GROUP):
                pre_p[zz] = total
                total = span[zz] * total + end[zz]

        to_parts(end_e, s1e, total, e1_copy)
        spans_on()
        from_parts(end_e, s1e, e1_send, e1_recv)
        e = s1e[0]
        for p in range(1, NP):
            e = s1q[p] * e + s1e[p]
        slab_e[...] = e
        for yy in range(1, NY):
            @pl.when(yy > y)
            def _():
                ye_copy(yy).start()

        cacc[...] = jnp.zeros((UP, LANES), F32)
        for yy in range(NY - 1):
            @pl.when(yy < y)
            def _():
                rcopy(slab_q, yq.at[yy], yq_send.at[yy], yq_recv.at[yy], at_y(yy)).wait_recv()
                rcopy(slab_e, ye.at[yy], ye_send.at[yy], ye_recv.at[yy], at_y(yy)).wait_recv()
                cacc[...] = yq[yy] * cacc[...] + ye[yy]

        start = cacc[...]
        for p in range(NP):
            @pl.when(line == p)
            def _():
                cbuf[p] = start

            @pl.when(line != p)
            def _():
                cst[p] = start
                c_copy(p).start()

            start = s1q[p] * start + s1e[p]
        from_parts(cst, cbuf, c_send, c_recv)

        def r_copy(zz):
            return rcopy(rsrc.at[zz], rbuf.at[tile], r_send.at[zz], r_recv.at[tile], at_z(zz))

        carry_in = jnp.concatenate([cbuf[p] for p in range(NP)], axis=0)
        pad = jnp.zeros((2 * LANES - USERS, LANES), BF16)

        def give(i, carry):
            blocks = [i * GROUP + j for j in range(GROUP)]
            for zz in blocks:
                states = (pre_p[zz] + pre_q[zz] * carry_in).astype(BF16)
                rsrc[zz] = dot(mt[zz], jnp.concatenate([states, pad], axis=0)).astype(BF16)
            for zz in blocks:
                @pl.when(zz == z)
                def _():
                    rbuf[tile] = rsrc[zz]

                @pl.when((zz > z) & ((lax.rem(zz, 4) == 3) | (zz >= 10)))
                def _():
                    pl.semaphore_wait(ready.at[zz], 1)

                @pl.when(zz != z)
                def _():
                    r_copy(zz).start()

            return carry

        lax.fori_loop(0, NZ // GROUP, give, 0)

        for p in range(NP):
            @pl.when(line != p)
            def _():
                q1_copy(p).wait_send()
                e1_copy(p).wait_send()
                c_copy(p).wait_send()
        for yy in range(1, NY):
            @pl.when(yy > y)
            def _():
                yq_copy(yy).wait_send()
                ye_copy(yy).wait_send()

    wcopies[3].wait()
    squares = jnp.zeros((ROWS, LANES), F32)
    for t in range(0, NT, 2):
        parts = []
        for u in (t, t + 1):
            zt = u + u // 3

            @pl.when(z != zt)
            def _():
                rcopy(rsrc.at[0], rbuf.at[u], r_send.at[0], r_recv.at[u], at_z(zt)).wait_recv()

            h = grow[u] * (xloc[u] + rbuf[u].astype(F32))
            squares = squares + h * h
            parts.append((h * sgate[u]).astype(BF16))
        prod = dot(jnp.concatenate(parts, axis=1), wo[LANES * t : LANES * (t + 2), :])
        if t == 0:
            acc[...] = prod
        else:
            acc[...] += prod
    mean_h = jnp.sum(squares, axis=1, keepdims=True) * (1.0 / full)
    out_ref[...] = (ev_ref[...].astype(F32) + acc[...] * lax.rsqrt(mean_h + 1e-6)).astype(BF16)

    for t in range(NT):
        zt = t + t // 3

        @pl.when(z != zt)
        def _():
            id_copy(t, zt).wait_send()
            v_copy(t, zt).wait_send()

    @pl.when(holder)
    def _():
        for zz in range(NZ):
            @pl.when(z != zz)
            def _():
                rcopy(rsrc.at[zz], rbuf.at[tile], r_send.at[zz], r_recv.at[tile], at_z(zz)).wait_send()


def on_device(NC, NX, NY, events, user_ids, session_break, in_gain, in_weight, decay_rates, keep_factor, out_gain, out_weight):
    NP = NC * NX
    UP = USERS // NP
    D = NT * LANES
    vmem = pl.BlockSpec(memory_space=pltpu.VMEM)
    hbm = pl.BlockSpec(memory_space=pl.ANY)
    V = pltpu.VMEM
    dma = lambda *n: pltpu.SemaphoreType.DMA(n)
    return pl.pallas_call(
        functools.partial(kernel, NC, NX, NY),
        out_shape=jax.ShapeDtypeStruct((ROWS, D), BF16),
        in_specs=[hbm] * 9,
        out_specs=vmem,
        scratch_shapes=[
            V((ROWS, D), BF16), V((1, ROWS), jnp.int32), V((1, ROWS), jnp.int32),
            V((1, D), F32), V((1, D), F32), V((1, D), F32), V((1, D), F32),
            V((2, D, D // 2), BF16), V((D, D), BF16), V((D, D), BF16),
            V((NT, ROWS, LANES), BF16), V((8, LANES), F32), V((NZ, 8, LANES), F32),
            V((NZ, ROWS, LANES), BF16), V((NZ, ROWS, 2 * LANES), BF16), V((NZ, USERS, 2 * LANES), BF16),
            V((NZ, ROWS, LANES), F32), V((NZ, USERS, LANES), F32), V((NZ + 1, USERS, LANES), F32),
            V((NZ, USERS, LANES), F32), V((NZ, USERS, LANES), F32),
            V((NP, UP, LANES), F32), V((NP, UP, LANES), F32), V((NP, UP, LANES), F32), V((NP, UP, LANES), F32),
            V((UP, LANES), F32), V((UP, LANES), F32), V((NY, UP, LANES), F32), V((NY, UP, LANES), F32),
            V((NP, UP, LANES), F32), V((NP, UP, LANES), F32), V((UP, LANES), F32),
            V((NZ, ROWS, LANES), BF16), V((NT, ROWS, LANES), BF16),
            V((NT, ROWS, LANES), F32), V((NT, ROWS, LANES), F32), V((NT, ROWS, LANES), F32),
            V((ROWS, D), F32), V((1, D), F32),
            dma(7), dma(4), dma(NT), dma(NZ), dma(NT), dma(NZ), dma(NP), dma(NP), dma(NP), dma(NP),
            dma(NY), dma(NY), dma(NY), dma(NY), dma(NP), dma(NP), dma(NZ), dma(NT),
            pltpu.SemaphoreType.REGULAR((NZ,)), pltpu.SemaphoreType.REGULAR, pltpu.SemaphoreType.REGULAR,
        ],
        compiler_params=pltpu.CompilerParams(
            collective_id=0, has_side_effects=True, vmem_limit_bytes=60 * 1024 * 1024
        ),
    )(
        events, user_ids.reshape(1, ROWS), session_break.reshape(1, ROWS),
        in_gain.reshape(1, D), decay_rates.reshape(1, D), keep_factor.reshape(1, D),
        out_gain.reshape(1, D), in_weight, out_weight,
    )


def solution(mesh):
    groups, shards = mesh.shape["grp"], mesh.shape["shard"]
    NC = 2 if groups % 2 == 0 else 1
    body = functools.partial(on_device, NC, shards // NZ, groups // NC)
    both = P(("grp", "shard"))
    return jax.shard_map(
        body,
        mesh=mesh,
        in_specs=(P(("grp", "shard"), None), both, both, P(), P(), P(), P(), P(), P()),
        out_specs=P(("grp", "shard"), None),
        check_vma=False,
    )
```

```python
import functools

import jax
import jax.numpy as jnp
from jax import lax
from jax.experimental import pallas as pl
from jax.experimental.pallas import tpu as pltpu
from jax.sharding import PartitionSpec as P

F32, BF16 = jnp.float32, jnp.bfloat16
MESH = pl.DeviceIdType.MESH
NZ = 12
NT = 8
LANES = 128
ROWS = 128
USERS = 192
GROUP = 4


def dot(a, b):
    return jnp.dot(a, b, preferred_element_type=F32)


def decay_of(counts, rate, log_keep):
    breaks = jnp.floor(counts * (1.0 / 16.0))
    return log_keep * breaks - rate * (counts - 16.0 * breaks)


def kernel(
    NC, NX, NY,
    ev_hbm, ids_hbm, brk_hbm, in_gain_hbm, rate_hbm, keep_hbm, out_gain_hbm, w_in, w_out,
    out_ref,
    ev_ref, ids_ref, brk_ref, in_gain_ref, rate_ref, keep_ref, out_gain_ref,
    wv, wg, wo, vt, id_src, idb, vbuf, mt, mem, dcy, span, pre_q, pre_p, end,
    end_e, end_q, s1e, s1q, slab_e, slab_q, ye, yq, cst, cbuf, cacc,
    rsrc, rbuf, xloc, grow, sgate, acc, lk_ref,
    op_sem, w_sem, id_send, id_recv, v_send, v_recv, q1_send, q1_recv, e1_send, e1_recv,
    yq_send, yq_recv, ye_send, ye_recv, c_send, c_recv, r_send, r_recv, ready, lines, go,
):
    NP = NC * NX
    UP = USERS // NP
    g, s = lax.axis_index("grp"), lax.axis_index("shard")
    y, c = lax.div(g, NC), lax.rem(g, NC)
    x, z = lax.div(s, NZ), lax.rem(s, NZ)
    line = c * NX + x
    holder = (lax.rem(z, 4) < 3) & (z < 10)
    tile = z - lax.div(z, 4)

    def at_z(zz):
        return (g, x * NZ + zz)

    def at_line(p):
        return (y * NC + p // NX, (p % NX) * NZ + z)

    def at_y(yy):
        return (yy * NC + c, s)

    def rcopy(src, dst, ss, rs, dev):
        return pltpu.make_async_remote_copy(
            src_ref=src, dst_ref=dst, send_sem=ss, recv_sem=rs, device_id=dev, device_id_type=MESH
        )

    ocopies = [
        pltpu.make_async_copy(src, dst, op_sem.at[i])
        for i, (src, dst) in enumerate((
            (ids_hbm, ids_ref), (brk_hbm, brk_ref), (ev_hbm, ev_ref), (in_gain_hbm, in_gain_ref),
            (rate_hbm, rate_ref), (keep_hbm, keep_ref), (out_gain_hbm, out_gain_ref),
        ))
    ]
    for cp in ocopies:
        cp.start()
    half = NT * LANES // 2
    full = NT * LANES
    wcopies = [
        pltpu.make_async_copy(w_in.at[:, pl.ds(full, half)], wv.at[0], w_sem.at[0]),
        pltpu.make_async_copy(w_in.at[:, pl.ds(full + half, half)], wv.at[1], w_sem.at[1]),
        pltpu.make_async_copy(w_in.at[:, pl.ds(0, full)], wg, w_sem.at[2]),
        pltpu.make_async_copy(w_out, wo, w_sem.at[3]),
    ]
    for cp in wcopies[:2]:
        cp.start()

    barrier = pltpu.get_barrier_semaphore()
    for zz in range(1, NZ):
        @pl.when(z < zz)
        def _():
            pl.semaphore_signal(barrier, inc=1, device_id=at_z(zz), device_id_type=MESH)

    def tell_peers(sem):
        for d in range(1, NP):
            p = lax.rem(line + d, NP)
            peer = (y * NC + lax.div(p, NX), lax.rem(p, NX) * NZ + z)
            pl.semaphore_signal(sem, inc=1, device_id=peer, device_id_type=MESH)
        for d in range(1, NY):
            pl.semaphore_signal(sem, inc=1, device_id=at_y(lax.rem(y + d, NY)), device_id_type=MESH)

    peers = NP - 1 + NY - 1

    @pl.when(z == 0)
    def _():
        tell_peers(barrier)

    @pl.when(z == 0)
    def _():
        pl.semaphore_wait(barrier, peers)

    @pl.when(z > 0)
    def _():
        pl.semaphore_wait(barrier, z)

    for zz in range(NZ - 1):
        @pl.when((z > zz) & (z > zz if zz % 4 < 3 and zz < 10 else holder))
        def _():
            pl.semaphore_signal(ready.at[z], inc=1, device_id=at_z(zz), device_id_type=MESH)

    for cp in ocopies[:2]:
        cp.wait()
    idr = ids_ref[...].astype(F32)
    brk = brk_ref[...].astype(F32)
    id_src[...] = jnp.concatenate([idr, brk, jnp.zeros((6, LANES), F32)], axis=0)

    def id_copy(t, zt):
        return rcopy(id_src, idb.at[z], id_send.at[t], id_recv.at[z], at_z(zt))

    def v_copy(t, zt):
        return rcopy(vt.at[t], vbuf.at[z], v_send.at[t], v_recv.at[z], at_z(zt))

    for t in range(NT):
        zt = t + t // 3

        @pl.when(z == zt)
        def _():
            idb[z] = id_src[...]

        @pl.when(z > zt)
        def _():
            id_copy(t, zt).start()

    for cp in ocopies[2:]:
        cp.wait()
    lk_ref[...] = jnp.log(keep_ref[...])
    ev = ev_ref[...].astype(F32)
    mean = jnp.sum(ev * ev, axis=1, keepdims=True) * (1.0 / full)
    normed = (ev * lax.rsqrt(mean + 1e-6) * in_gain_ref[...]).astype(BF16)
    for grp in range(2):
        wcopies[grp].wait()
        if grp == 1:
            for cp in wcopies[2:]:
                cp.start()
        v = dot(normed, wv[grp]).astype(BF16)
        for k in range(4):
            vt[4 * grp + k] = v[:, LANES * k : LANES * (k + 1)]

    def send_values(order):
        for t in order:
            zt = t + t // 3

            @pl.when(z < zt)
            def _():
                pl.semaphore_wait(ready.at[zt], 1)
                id_copy(t, zt).start()

            @pl.when(z == zt)
            def _():
                vbuf[z] = vt[t]

            @pl.when(z != zt)
            def _():
                v_copy(t, zt).start()

    @pl.when(z < 7)
    def _():
        send_values(range(NT))

    @pl.when(z >= 7)
    def _():
        send_values((0, 5, 1, 4, 2, 3, 7, 6))

    @pl.when(z == 0)
    def _():
        tell_peers(lines)

    sub = lax.broadcasted_iota(jnp.int32, (ROWS, LANES), 0)
    lane = lax.broadcasted_iota(jnp.int32, (ROWS, LANES), 1)
    ones = jnp.ones((LANES, LANES), BF16)

    wcopies[2].wait()
    weight = 1.0 + 16.0 * brk
    col = dot(jnp.where(sub == lane, idr, 0.0).astype(BF16), ones)
    upto = (col == idr) & (lane <= sub)
    counts = dot(jnp.where(upto, weight, 0.0).astype(BF16), ones)
    within = upto.astype(F32).astype(BF16)
    within = jnp.concatenate([within, within], axis=1)
    breaks = jnp.floor(counts * (1.0 / 16.0))
    events_of = counts - 16.0 * breaks
    for t in range(NT):
        cols = slice(LANES * t, LANES * (t + 1))
        level = lk_ref[:, cols] * breaks - rate_ref[:, cols] * events_of
        grow[t] = jnp.exp(level)
        scaled = jnp.exp(-level) * vt[t].astype(F32)
        hi = scaled.astype(BF16)
        lo = (scaled - hi.astype(F32)).astype(BF16)
        xloc[t] = dot(within, jnp.concatenate([hi, lo], axis=0))
    gate = dot(normed, wg[...]).astype(BF16).astype(F32)
    gate = out_gain_ref[...] * (gate / (1.0 + jnp.exp(-gate)))
    for t in range(NT):
        sgate[t] = gate[:, LANES * t : LANES * (t + 1)]

    @pl.when(z == 0)
    def _():
        pl.semaphore_wait(lines, peers)
        for t in range(1, NT):
            pl.semaphore_signal(go, inc=1, device_id=at_z(t + t // 3), device_id_type=MESH)

    @pl.when(holder)
    def _():
        at = pl.ds(pl.multiple_of(tile * LANES, LANES), LANES)
        rate, log_keep = rate_ref[:, at], lk_ref[:, at]
        ones2 = jnp.ones((LANES, 2 * LANES), BF16)
        lane2 = lax.broadcasted_iota(jnp.int32, (ROWS, 2 * LANES), 1).astype(F32)
        usub = lax.broadcasted_iota(jnp.int32, (USERS, LANES), 0).astype(F32)

        pre_q[0] = jnp.ones((USERS, LANES), F32)

        def prep(zz):
            info = idb[zz]
            row, weight = info[0:1], 1.0 + 16.0 * info[1:2]
            col = dot(jnp.where(sub == lane, row, 0.0).astype(BF16), ones2)
            mt[zz] = (col == lane2).astype(F32).astype(BF16)
            after = jnp.where((col[:, :LANES] == row) & (lane > sub), weight, 0.0).astype(BF16)
            dcy[zz] = jnp.exp(decay_of(dot(after, ones), rate, log_keep))
            own = usub == row
            own_b = own.astype(F32).astype(BF16)
            mem[zz] = jnp.concatenate([own_b, own_b], axis=1)
            sp = jnp.exp(decay_of(dot(jnp.where(own, weight, 0.0).astype(BF16), ones), rate, log_keep))
            span[zz] = sp
            pre_q[zz + 1] = pre_q[zz] * sp

        def prep_some(i, carry):
            for j in range(GROUP):
                zz = i * GROUP + j

                @pl.when(z != zz)
                def _():
                    rcopy(id_src, idb.at[zz], id_send.at[0], id_recv.at[zz], at_z(zz)).wait_recv()

            for j in range(GROUP):
                prep(i * GROUP + j)
            return carry

        lax.fori_loop(0, NZ // GROUP, prep_some, 0)

        def q1_copy(p):
            return rcopy(end_q.at[p], s1q.at[line], q1_send.at[p], q1_recv.at[line], at_line(p))

        def e1_copy(p):
            return rcopy(end_e.at[p], s1e.at[line], e1_send.at[p], e1_recv.at[line], at_line(p))

        def c_copy(p):
            return rcopy(cst.at[p], cbuf.at[line], c_send.at[p], c_recv.at[line], at_line(p))

        def yq_copy(yy):
            return rcopy(slab_q, yq.at[y], yq_send.at[yy], yq_recv.at[y], at_y(yy))

        def ye_copy(yy):
            return rcopy(slab_e, ye.at[y], ye_send.at[yy], ye_recv.at[y], at_y(yy))

        def to_parts(src, dst, value, copy):
            for p in range(NP):
                part = value[UP * p : UP * (p + 1)]

                @pl.when(line == p)
                def _():
                    dst[p] = part

                @pl.when(line != p)
                def _():
                    src[p] = part
                    copy(p).start()

        def from_parts(src, dst, ss, rs):
            for p in range(NP):
                @pl.when(line != p)
                def _():
                    rcopy(src.at[p], dst.at[p], ss.at[p], rs.at[p], at_line(p)).wait_recv()

        def spans_on():
            from_parts(end_q, s1q, q1_send, q1_recv)
            q = s1q[0]
            for p in range(1, NP):
                q = q * s1q[p]
            slab_q[...] = q
            for yy in range(NY - 1, 0, -1):
                @pl.when(yy > y)
                def _():
                    yq_copy(yy).start()

        def ends(zz):
            w = dcy[zz] * vbuf[zz].astype(F32)
            hi = w.astype(BF16)
            lo = (w - hi.astype(F32)).astype(BF16)
            end[zz] = dot(mem[zz], jnp.concatenate([hi, lo], axis=0))

        total = jnp.zeros((USERS, LANES), F32)
        for i in range(0, NZ, GROUP):
            if i + GROUP == NZ:
                @pl.when(z > 0)
                def _():
                    pl.semaphore_wait(go, 1)

                to_parts(end_q, s1q, pre_q[NZ], q1_copy)
            for zz in range(i, i + GROUP):
                @pl.when(z != zz)
                def _():
                    rcopy(vt.at[0], vbuf.at[zz], v_send.at[0], v_recv.at[zz], at_z(zz)).wait_recv()

            for zz in range(i, i + GROUP):
                ends(zz)
            for zz in range(i, i + GROUP):
                pre_p[zz] = total
                total = span[zz] * total + end[zz]

        to_parts(end_e, s1e, total, e1_copy)
        spans_on()
        from_parts(end_e, s1e, e1_send, e1_recv)
        e = s1e[0]
        for p in range(1, NP):
            e = s1q[p] * e + s1e[p]
        slab_e[...] = e
        for yy in range(NY - 1, 0, -1):
            @pl.when(yy > y)
            def _():
                ye_copy(yy).start()

        cacc[...] = jnp.zeros((UP, LANES), F32)
        for yy in range(NY - 1):
            @pl.when(yy < y)
            def _():
                rcopy(slab_q, yq.at[yy], yq_send.at[yy], yq_recv.at[yy], at_y(yy)).wait_recv()
                rcopy(slab_e, ye.at[yy], ye_send.at[yy], ye_recv.at[yy], at_y(yy)).wait_recv()
                cacc[...] = yq[yy] * cacc[...] + ye[yy]

        start = cacc[...]
        for p in range(NP):
            @pl.when(line == p)
            def _():
                cbuf[p] = start

            @pl.when(line != p)
            def _():
                cst[p] = start
                c_copy(p).start()

            start = s1q[p] * start + s1e[p]
        from_parts(cst, cbuf, c_send, c_recv)

        def r_copy(zz):
            return rcopy(rsrc.at[zz], rbuf.at[tile], r_send.at[zz], r_recv.at[tile], at_z(zz))

        carry_in = jnp.concatenate([cbuf[p] for p in range(NP)], axis=0)
        pad = jnp.zeros((2 * LANES - USERS, LANES), BF16)

        def give(blocks):
            for zz in blocks:
                states = (pre_p[zz] + pre_q[zz] * carry_in).astype(BF16)
                rsrc[zz] = dot(mt[zz], jnp.concatenate([states, pad], axis=0)).astype(BF16)
            for zz in blocks:
                @pl.when(zz == z)
                def _():
                    rbuf[tile] = rsrc[zz]

                if zz % 4 == 3 or zz >= 10:
                    @pl.when(zz > z)
                    def _():
                        pl.semaphore_wait(ready.at[zz], 1)

                @pl.when(zz != z)
                def _():
                    r_copy(zz).start()

        for blocks in ((0,), (1, 2), (3, 4, 5), (6, 7, 8), (9, 10, 11)):
            give(blocks)

        for p in range(NP):
            @pl.when(line != p)
            def _():
                q1_copy(p).wait_send()
                e1_copy(p).wait_send()
                c_copy(p).wait_send()
        for yy in range(1, NY):
            @pl.when(yy > y)
            def _():
                yq_copy(yy).wait_send()
                ye_copy(yy).wait_send()

    wcopies[3].wait()
    squares = jnp.zeros((ROWS, LANES), F32)
    for t in range(0, NT, 2):
        parts = []
        for u in (t, t + 1):
            zt = u + u // 3

            @pl.when(z != zt)
            def _():
                rcopy(rsrc.at[0], rbuf.at[u], r_send.at[0], r_recv.at[u], at_z(zt)).wait_recv()

            h = grow[u] * (xloc[u] + rbuf[u].astype(F32))
            squares = squares + h * h
            parts.append((h * sgate[u]).astype(BF16))
        prod = dot(jnp.concatenate(parts, axis=1), wo[LANES * t : LANES * (t + 2), :])
        if t == 0:
            acc[...] = prod
        else:
            acc[...] += prod
    mean_h = jnp.sum(squares, axis=1, keepdims=True) * (1.0 / full)
    out_ref[...] = acc[...] * lax.rsqrt(mean_h + 1e-6)

    for t in range(NT):
        zt = t + t // 3

        @pl.when(z != zt)
        def _():
            id_copy(t, zt).wait_send()
            v_copy(t, zt).wait_send()

    @pl.when(holder)
    def _():
        for zz in range(NZ):
            @pl.when(z != zz)
            def _():
                rcopy(rsrc.at[zz], rbuf.at[tile], r_send.at[zz], r_recv.at[tile], at_z(zz)).wait_send()


def on_device(NC, NX, NY, events, user_ids, session_break, in_gain, in_weight, decay_rates, keep_factor, out_gain, out_weight):
    NP = NC * NX
    UP = USERS // NP
    D = NT * LANES
    vmem = pl.BlockSpec(memory_space=pltpu.VMEM)
    hbm = pl.BlockSpec(memory_space=pl.ANY)
    V = pltpu.VMEM
    dma = lambda *n: pltpu.SemaphoreType.DMA(n)
    part = pl.pallas_call(
        functools.partial(kernel, NC, NX, NY),
        out_shape=jax.ShapeDtypeStruct((ROWS, D), F32),
        in_specs=[hbm] * 9,
        out_specs=vmem,
        scratch_shapes=[
            V((ROWS, D), BF16), V((1, ROWS), jnp.int32), V((1, ROWS), jnp.int32),
            V((1, D), F32), V((1, D), F32), V((1, D), F32), V((1, D), F32),
            V((2, D, D // 2), BF16), V((D, D), BF16), V((D, D), BF16),
            V((NT, ROWS, LANES), BF16), V((8, LANES), F32), V((NZ, 8, LANES), F32),
            V((NZ, ROWS, LANES), BF16), V((NZ, ROWS, 2 * LANES), BF16), V((NZ, USERS, 2 * LANES), BF16),
            V((NZ, ROWS, LANES), F32), V((NZ, USERS, LANES), F32), V((NZ + 1, USERS, LANES), F32),
            V((NZ, USERS, LANES), F32), V((NZ, USERS, LANES), F32),
            V((NP, UP, LANES), F32), V((NP, UP, LANES), F32), V((NP, UP, LANES), F32), V((NP, UP, LANES), F32),
            V((UP, LANES), F32), V((UP, LANES), F32), V((NY, UP, LANES), F32), V((NY, UP, LANES), F32),
            V((NP, UP, LANES), F32), V((NP, UP, LANES), F32), V((UP, LANES), F32),
            V((NZ, ROWS, LANES), BF16), V((NT, ROWS, LANES), BF16),
            V((NT, ROWS, LANES), F32), V((NT, ROWS, LANES), F32), V((NT, ROWS, LANES), F32),
            V((ROWS, D), F32), V((1, D), F32),
            dma(7), dma(4), dma(NT), dma(NZ), dma(NT), dma(NZ), dma(NP), dma(NP), dma(NP), dma(NP),
            dma(NY), dma(NY), dma(NY), dma(NY), dma(NP), dma(NP), dma(NZ), dma(NT),
            pltpu.SemaphoreType.REGULAR((NZ,)), pltpu.SemaphoreType.REGULAR, pltpu.SemaphoreType.REGULAR,
        ],
        compiler_params=pltpu.CompilerParams(
            collective_id=0, has_side_effects=True, vmem_limit_bytes=60 * 1024 * 1024
        ),
    )(
        events, user_ids.reshape(1, ROWS), session_break.reshape(1, ROWS),
        in_gain.reshape(1, D), decay_rates.reshape(1, D), keep_factor.reshape(1, D),
        out_gain.reshape(1, D), in_weight, out_weight,
    )
    return (events.astype(F32) + part).astype(BF16)


def solution(mesh):
    groups, shards = mesh.shape["grp"], mesh.shape["shard"]
    NC = 2 if groups % 2 == 0 else 1
    body = functools.partial(on_device, NC, shards // NZ, groups // NC)
    both = P(("grp", "shard"))
    return jax.shard_map(
        body,
        mesh=mesh,
        in_specs=(P(("grp", "shard"), None), both, both, P(), P(), P(), P(), P(), P()),
        out_specs=P(("grp", "shard"), None),
        check_vma=False,
    )
```

```python
import functools

import jax
import jax.numpy as jnp
from jax import lax
from jax.experimental import pallas as pl
from jax.experimental.pallas import tpu as pltpu
from jax.sharding import PartitionSpec as P

F32, BF16 = jnp.float32, jnp.bfloat16
MESH = pl.DeviceIdType.MESH
NZ = 12
NT = 8
LANES = 128
ROWS = 128
USERS = 192
GROUP = 4


def dot(a, b):
    return jnp.dot(a, b, preferred_element_type=F32)


def decay_of(counts, rate, log_keep):
    breaks = jnp.floor(counts * (1.0 / 16.0))
    return log_keep * breaks - rate * (counts - 16.0 * breaks)


def kernel(
    NC, NX, NY,
    ev_hbm, ids_hbm, brk_hbm, in_gain_hbm, rate_hbm, keep_hbm, out_gain_hbm, w_in, w_out,
    out_ref,
    ev_ref, ids_ref, brk_ref, in_gain_ref, rate_ref, keep_ref, out_gain_ref,
    wv, wg, wo, vt, id_src, idb, vbuf, mt, mem, dcy, span, pre_q, pre_p, end,
    end_e, end_q, s1e, s1q, slab_e, slab_q, ye, yq, cst, cbuf, cacc,
    rsrc, rbuf, xloc, grow, sgate, acc, lk_ref,
    op_sem, w_sem, id_send, id_recv, v_send, v_recv, q1_send, q1_recv, e1_send, e1_recv,
    yq_send, yq_recv, ye_send, ye_recv, c_send, c_recv, r_send, r_recv, ready, lines, go,
):
    NP = NC * NX
    UP = USERS // NP
    g, s = lax.axis_index("grp"), lax.axis_index("shard")
    y, c = lax.div(g, NC), lax.rem(g, NC)
    x, z = lax.div(s, NZ), lax.rem(s, NZ)
    line = c * NX + x
    holder = (lax.rem(z, 4) < 3) & (z < 10)
    tile = z - lax.div(z, 4)

    def at_z(zz):
        return (g, x * NZ + zz)

    def at_line(p):
        return (y * NC + p // NX, (p % NX) * NZ + z)

    def at_y(yy):
        return (yy * NC + c, s)

    def rcopy(src, dst, ss, rs, dev):
        return pltpu.make_async_remote_copy(
            src_ref=src, dst_ref=dst, send_sem=ss, recv_sem=rs, device_id=dev, device_id_type=MESH
        )

    ocopies = [
        pltpu.make_async_copy(src, dst, op_sem.at[i])
        for i, (src, dst) in enumerate((
            (ids_hbm, ids_ref), (brk_hbm, brk_ref), (ev_hbm, ev_ref), (in_gain_hbm, in_gain_ref),
            (rate_hbm, rate_ref), (keep_hbm, keep_ref), (out_gain_hbm, out_gain_ref),
        ))
    ]
    for cp in ocopies:
        cp.start()
    half = NT * LANES // 2
    full = NT * LANES
    wcopies = [
        pltpu.make_async_copy(w_in.at[:, pl.ds(full, half)], wv.at[0], w_sem.at[0]),
        pltpu.make_async_copy(w_in.at[:, pl.ds(full + half, half)], wv.at[1], w_sem.at[1]),
        pltpu.make_async_copy(w_in.at[:, pl.ds(0, full)], wg, w_sem.at[2]),
        pltpu.make_async_copy(w_out, wo, w_sem.at[3]),
    ]
    for cp in wcopies[:2]:
        cp.start()

    barrier = pltpu.get_barrier_semaphore()
    for zz in range(1, NZ):
        @pl.when(z < zz)
        def _():
            pl.semaphore_signal(barrier, inc=1, device_id=at_z(zz), device_id_type=MESH)

    def tell_peers(sem):
        for d in range(1, NP):
            p = lax.rem(line + d, NP)
            peer = (y * NC + lax.div(p, NX), lax.rem(p, NX) * NZ + z)
            pl.semaphore_signal(sem, inc=1, device_id=peer, device_id_type=MESH)
        for d in range(1, NY):
            pl.semaphore_signal(sem, inc=1, device_id=at_y(lax.rem(y + d, NY)), device_id_type=MESH)

    peers = NP - 1 + NY - 1

    @pl.when(z == 0)
    def _():
        tell_peers(barrier)

    for cp in ocopies[:2]:
        cp.wait()
    idr = ids_ref[...].astype(F32)
    brk = brk_ref[...].astype(F32)
    id_src[...] = jnp.concatenate([idr, brk, jnp.zeros((6, LANES), F32)], axis=0)

    @pl.when(z == 0)
    def _():
        pl.semaphore_wait(barrier, peers)

    @pl.when(z > 0)
    def _():
        pl.semaphore_wait(barrier, z)

    for zz in range(NZ - 1):
        @pl.when((z > zz) & (z > zz if zz % 4 < 3 and zz < 10 else holder))
        def _():
            pl.semaphore_signal(ready.at[z], inc=1, device_id=at_z(zz), device_id_type=MESH)

    def id_copy(t, zt):
        return rcopy(id_src, idb.at[z], id_send.at[t], id_recv.at[z], at_z(zt))

    def v_copy(t, zt):
        return rcopy(vt.at[t], vbuf.at[z], v_send.at[t], v_recv.at[z], at_z(zt))

    for t in range(NT):
        zt = t + t // 3

        @pl.when(z == zt)
        def _():
            idb[z] = id_src[...]

        @pl.when(z > zt)
        def _():
            id_copy(t, zt).start()

    for cp in ocopies[2:]:
        cp.wait()
    lk_ref[...] = jnp.log(keep_ref[...])
    ev = ev_ref[...].astype(F32)
    mean = jnp.sum(ev * ev, axis=1, keepdims=True) * (1.0 / full)
    normed = (ev * lax.rsqrt(mean + 1e-6) * in_gain_ref[...]).astype(BF16)
    for grp in range(2):
        wcopies[grp].wait()
        if grp == 1:
            for cp in wcopies[2:]:
                cp.start()
        v = dot(normed, wv[grp]).astype(BF16)
        for t in range(4):
            vt[4 * grp + t] = v[:, LANES * t : LANES * (t + 1)]

    for t in range(NT):
        zt = t + t // 3

        @pl.when(z < zt)
        def _():
            pl.semaphore_wait(ready.at[zt], 1)
            id_copy(t, zt).start()

        @pl.when(z == zt)
        def _():
            vbuf[z] = vt[t]

        @pl.when(z != zt)
        def _():
            v_copy(t, zt).start()

    @pl.when(z == 0)
    def _():
        tell_peers(lines)

    sub = lax.broadcasted_iota(jnp.int32, (ROWS, LANES), 0)
    lane = lax.broadcasted_iota(jnp.int32, (ROWS, LANES), 1)
    ones = jnp.ones((LANES, LANES), BF16)

    wcopies[2].wait()
    weight = 1.0 + 16.0 * brk
    col = dot(jnp.where(sub == lane, idr, 0.0).astype(BF16), ones)
    upto = (col == idr) & (lane <= sub)
    counts = dot(jnp.where(upto, weight, 0.0).astype(BF16), ones)
    within = upto.astype(F32).astype(BF16)
    within = jnp.concatenate([within, within], axis=1)
    breaks = jnp.floor(counts * (1.0 / 16.0))
    events_of = counts - 16.0 * breaks
    for t in range(NT):
        cols = slice(LANES * t, LANES * (t + 1))
        level = lk_ref[:, cols] * breaks - rate_ref[:, cols] * events_of
        grow[t] = jnp.exp(level)
        scaled = jnp.exp(-level) * vt[t].astype(F32)
        hi = scaled.astype(BF16)
        lo = (scaled - hi.astype(F32)).astype(BF16)
        xloc[t] = dot(within, jnp.concatenate([hi, lo], axis=0))
    gate = dot(normed, wg[...]).astype(BF16).astype(F32)
    gate = out_gain_ref[...] * (gate / (1.0 + jnp.exp(-gate)))
    for t in range(NT):
        sgate[t] = gate[:, LANES * t : LANES * (t + 1)]

    @pl.when(z == 0)
    def _():
        pl.semaphore_wait(lines, peers)
        for t in range(1, NT):
            pl.semaphore_signal(go, inc=1, device_id=at_z(t + t // 3), device_id_type=MESH)

    @pl.when(holder)
    def _():
        at = pl.ds(pl.multiple_of(tile * LANES, LANES), LANES)
        rate, log_keep = rate_ref[:, at], lk_ref[:, at]
        ones2 = jnp.ones((LANES, 2 * LANES), BF16)
        lane2 = lax.broadcasted_iota(jnp.int32, (ROWS, 2 * LANES), 1).astype(F32)
        usub = lax.broadcasted_iota(jnp.int32, (USERS, LANES), 0).astype(F32)

        pre_q[0] = jnp.ones((USERS, LANES), F32)

        def prep(zz):
            info = idb[zz]
            row, weight = info[0:1], 1.0 + 16.0 * info[1:2]
            col = dot(jnp.where(sub == lane, row, 0.0).astype(BF16), ones2)
            mt[zz] = (col == lane2).astype(F32).astype(BF16)
            after = jnp.where((col[:, :LANES] == row) & (lane > sub), weight, 0.0).astype(BF16)
            dcy[zz] = jnp.exp(decay_of(dot(after, ones), rate, log_keep))
            own = usub == row
            own_b = own.astype(F32).astype(BF16)
            mem[zz] = jnp.concatenate([own_b, own_b], axis=1)
            sp = jnp.exp(decay_of(dot(jnp.where(own, weight, 0.0).astype(BF16), ones), rate, log_keep))
            span[zz] = sp
            pre_q[zz + 1] = pre_q[zz] * sp

        def prep_some(i, carry):
            for j in range(GROUP):
                zz = i * GROUP + j

                @pl.when(z != zz)
                def _():
                    rcopy(id_src, idb.at[zz], id_send.at[0], id_recv.at[zz], at_z(zz)).wait_recv()

            for j in range(GROUP):
                prep(i * GROUP + j)
            return carry

        lax.fori_loop(0, NZ // GROUP, prep_some, 0)

        def q1_copy(p):
            return rcopy(end_q.at[p], s1q.at[line], q1_send.at[p], q1_recv.at[line], at_line(p))

        def e1_copy(p):
            return rcopy(end_e.at[p], s1e.at[line], e1_send.at[p], e1_recv.at[line], at_line(p))

        def c_copy(p):
            return rcopy(cst.at[p], cbuf.at[line], c_send.at[p], c_recv.at[line], at_line(p))

        def yq_copy(yy):
            return rcopy(slab_q, yq.at[y], yq_send.at[yy], yq_recv.at[y], at_y(yy))

        def ye_copy(yy):
            return rcopy(slab_e, ye.at[y], ye_send.at[yy], ye_recv.at[y], at_y(yy))

        def to_parts(src, dst, value, copy):
            for p in range(NP):
                part = value[UP * p : UP * (p + 1)]

                @pl.when(line == p)
                def _():
                    dst[p] = part

                @pl.when(line != p)
                def _():
                    src[p] = part
                    copy(p).start()

        def from_parts(src, dst, ss, rs):
            for p in range(NP):
                @pl.when(line != p)
                def _():
                    rcopy(src.at[p], dst.at[p], ss.at[p], rs.at[p], at_line(p)).wait_recv()

        def spans_on():
            from_parts(end_q, s1q, q1_send, q1_recv)
            q = s1q[0]
            for p in range(1, NP):
                q = q * s1q[p]
            slab_q[...] = q
            for yy in range(NY - 1, 0, -1):
                @pl.when(yy > y)
                def _():
                    yq_copy(yy).start()

        def ends(zz):
            w = dcy[zz] * vbuf[zz].astype(F32)
            hi = w.astype(BF16)
            lo = (w - hi.astype(F32)).astype(BF16)
            end[zz] = dot(mem[zz], jnp.concatenate([hi, lo], axis=0))

        total = jnp.zeros((USERS, LANES), F32)
        for i in range(0, NZ, GROUP):
            if i + GROUP == NZ:
                @pl.when(z > 0)
                def _():
                    pl.semaphore_wait(go, 1)

                to_parts(end_q, s1q, pre_q[NZ], q1_copy)
            for zz in range(i, i + GROUP):
                @pl.when(z != zz)
                def _():
                    rcopy(vt.at[0], vbuf.at[zz], v_send.at[0], v_recv.at[zz], at_z(zz)).wait_recv()

            for zz in range(i, i + GROUP):
                ends(zz)
            for zz in range(i, i + GROUP):
                pre_p[zz] = total
                total = span[zz] * total + end[zz]

        to_parts(end_e, s1e, total, e1_copy)
        spans_on()
        from_parts(end_e, s1e, e1_send, e1_recv)
        e = s1e[0]
        for p in range(1, NP):
            e = s1q[p] * e + s1e[p]
        slab_e[...] = e
        for yy in range(NY - 1, 0, -1):
            @pl.when(yy > y)
            def _():
                ye_copy(yy).start()

        cacc[...] = jnp.zeros((UP, LANES), F32)
        for yy in range(NY - 1):
            @pl.when(yy < y)
            def _():
                rcopy(slab_q, yq.at[yy], yq_send.at[yy], yq_recv.at[yy], at_y(yy)).wait_recv()
                rcopy(slab_e, ye.at[yy], ye_send.at[yy], ye_recv.at[yy], at_y(yy)).wait_recv()
                cacc[...] = yq[yy] * cacc[...] + ye[yy]

        start = cacc[...]
        for p in range(NP):
            @pl.when(line == p)
            def _():
                cbuf[p] = start

            @pl.when(line != p)
            def _():
                cst[p] = start
                c_copy(p).start()

            start = s1q[p] * start + s1e[p]
        from_parts(cst, cbuf, c_send, c_recv)

        def r_copy(zz):
            return rcopy(rsrc.at[zz], rbuf.at[tile], r_send.at[zz], r_recv.at[tile], at_z(zz))

        carry_in = jnp.concatenate([cbuf[p] for p in range(NP)], axis=0)
        pad = jnp.zeros((2 * LANES - USERS, LANES), BF16)

        def give(i, carry):
            blocks = [i * GROUP + j for j in range(GROUP)]
            for zz in blocks:
                states = (pre_p[zz] + pre_q[zz] * carry_in).astype(BF16)
                rsrc[zz] = dot(mt[zz], jnp.concatenate([states, pad], axis=0)).astype(BF16)
            for zz in blocks:
                @pl.when(zz == z)
                def _():
                    rbuf[tile] = rsrc[zz]

                @pl.when((zz > z) & ((lax.rem(zz, 4) == 3) | (zz >= 10)))
                def _():
                    pl.semaphore_wait(ready.at[zz], 1)

                @pl.when(zz != z)
                def _():
                    r_copy(zz).start()

            return carry

        lax.fori_loop(0, NZ // GROUP, give, 0)

        for p in range(NP):
            @pl.when(line != p)
            def _():
                q1_copy(p).wait_send()
                e1_copy(p).wait_send()
                c_copy(p).wait_send()
        for yy in range(1, NY):
            @pl.when(yy > y)
            def _():
                yq_copy(yy).wait_send()
                ye_copy(yy).wait_send()

    wcopies[3].wait()
    squares = jnp.zeros((ROWS, LANES), F32)
    for t in range(0, NT, 2):
        parts = []
        for u in (t, t + 1):
            zt = u + u // 3

            @pl.when(z != zt)
            def _():
                rcopy(rsrc.at[0], rbuf.at[u], r_send.at[0], r_recv.at[u], at_z(zt)).wait_recv()

            h = grow[u] * (xloc[u] + rbuf[u].astype(F32))
            squares = squares + h * h
            parts.append((h * sgate[u]).astype(BF16))
        prod = dot(jnp.concatenate(parts, axis=1), wo[LANES * t : LANES * (t + 2), :])
        if t == 0:
            acc[...] = prod
        else:
            acc[...] += prod
    mean_h = jnp.sum(squares, axis=1, keepdims=True) * (1.0 / full)
    out_ref[...] = (ev_ref[...].astype(F32) + acc[...] * lax.rsqrt(mean_h + 1e-6)).astype(BF16)

    for t in range(NT):
        zt = t + t // 3

        @pl.when(z != zt)
        def _():
            id_copy(t, zt).wait_send()
            v_copy(t, zt).wait_send()

    @pl.when(holder)
    def _():
        for zz in range(NZ):
            @pl.when(z != zz)
            def _():
                rcopy(rsrc.at[zz], rbuf.at[tile], r_send.at[zz], r_recv.at[tile], at_z(zz)).wait_send()


def on_device(NC, NX, NY, events, user_ids, session_break, in_gain, in_weight, decay_rates, keep_factor, out_gain, out_weight):
    NP = NC * NX
    UP = USERS // NP
    D = NT * LANES
    vmem = pl.BlockSpec(memory_space=pltpu.VMEM)
    hbm = pl.BlockSpec(memory_space=pl.ANY)
    V = pltpu.VMEM
    dma = lambda *n: pltpu.SemaphoreType.DMA(n)
    return pl.pallas_call(
        functools.partial(kernel, NC, NX, NY),
        out_shape=jax.ShapeDtypeStruct((ROWS, D), BF16),
        in_specs=[hbm] * 9,
        out_specs=vmem,
        scratch_shapes=[
            V((ROWS, D), BF16), V((1, ROWS), jnp.int32), V((1, ROWS), jnp.int32),
            V((1, D), F32), V((1, D), F32), V((1, D), F32), V((1, D), F32),
            V((2, D, D // 2), BF16), V((D, D), BF16), V((D, D), BF16),
            V((NT, ROWS, LANES), BF16), V((8, LANES), F32), V((NZ, 8, LANES), F32),
            V((NZ, ROWS, LANES), BF16), V((NZ, ROWS, 2 * LANES), BF16), V((NZ, USERS, 2 * LANES), BF16),
            V((NZ, ROWS, LANES), F32), V((NZ, USERS, LANES), F32), V((NZ + 1, USERS, LANES), F32),
            V((NZ, USERS, LANES), F32), V((NZ, USERS, LANES), F32),
            V((NP, UP, LANES), F32), V((NP, UP, LANES), F32), V((NP, UP, LANES), F32), V((NP, UP, LANES), F32),
            V((UP, LANES), F32), V((UP, LANES), F32), V((NY, UP, LANES), F32), V((NY, UP, LANES), F32),
            V((NP, UP, LANES), F32), V((NP, UP, LANES), F32), V((UP, LANES), F32),
            V((NZ, ROWS, LANES), BF16), V((NT, ROWS, LANES), BF16),
            V((NT, ROWS, LANES), F32), V((NT, ROWS, LANES), F32), V((NT, ROWS, LANES), F32),
            V((ROWS, D), F32), V((1, D), F32),
            dma(7), dma(4), dma(NT), dma(NZ), dma(NT), dma(NZ), dma(NP), dma(NP), dma(NP), dma(NP),
            dma(NY), dma(NY), dma(NY), dma(NY), dma(NP), dma(NP), dma(NZ), dma(NT),
            pltpu.SemaphoreType.REGULAR((NZ,)), pltpu.SemaphoreType.REGULAR, pltpu.SemaphoreType.REGULAR,
        ],
        compiler_params=pltpu.CompilerParams(
            collective_id=0, has_side_effects=True, vmem_limit_bytes=60 * 1024 * 1024
        ),
    )(
        events, user_ids.reshape(1, ROWS), session_break.reshape(1, ROWS),
        in_gain.reshape(1, D), decay_rates.reshape(1, D), keep_factor.reshape(1, D),
        out_gain.reshape(1, D), in_weight, out_weight,
    )


def solution(mesh):
    groups, shards = mesh.shape["grp"], mesh.shape["shard"]
    NC = 2 if groups % 2 == 0 else 1
    body = functools.partial(on_device, NC, shards // NZ, groups // NC)
    both = P(("grp", "shard"))
    return jax.shard_map(
        body,
        mesh=mesh,
        in_specs=(P(("grp", "shard"), None), both, both, P(), P(), P(), P(), P(), P()),
        out_specs=P(("grp", "shard"), None),
        check_vma=False,
    )
```
